256 devices in a mesh: lat: 8 (over y_lo, x), lon: 32 (over z, y_hi, core).
Axes of the slice: x: 4, y: 4 (y_hi: 2, y_lo: 2; y = y_hi * 2 + y_lo), z: 8, core: 2. Of those that a mesh axis runs over, the one named last changes fastest.
Arguments:
- tokens: bfloat16 [320, 768, 1024], P('lat', 'lon'), may hold values from -6 to 6
- qkv_weight: bfloat16 [1024, 3072], replicated, may hold values from -3 to 3, as said below
- proj_weight: bfloat16 [1024, 1024], replicated, may hold values from -0.1875 to 0.1875
Outputs:
- mixed: bfloat16 [320, 768, 1024], P('lat', 'lon')
The draws below stay inside these ranges and needn't reach their ends.
Inputs may be any that keep to these rules, and one draw needn't show every extreme that they name: `qkv_weight`: columns hold the query, key and value projections in that order, heads in order within each.
All inputs are finite; a program needn't handle non-finite values.
Results may differ from the reference program's by a relative error of at most 0.0047.
Values may be sent and summed in bfloat16 or wider, within the bound.
A program may use at most 128 MiB of HBM per device.

```python
import jax
import jax.numpy as jnp
from jax import lax

D = 1024
HEADS = 16
TH = 40
TW = 24
HALO = 2
HD = 64
ROWS = 320
COLS = 768
N_LAT = 8
N_LON = 32


def draw_qkv_weight(key, part):
    key = jax.random.fold_in(key, 7)
    base_key = jax.random.fold_in(key, 0)
    base = jnp.clip(jax.random.normal(base_key, (D, 3 * D), jnp.float32), -6.0, 6.0)
    unit = D ** (-0.5)
    return (base * unit).astype(jnp.bfloat16)


def steps_of(rng, dims, cuts, smallest, top_value):
    def one(dim, parts):
        steps = jax.random.uniform(jax.random.fold_in(jax.random.fold_in(rng, 6), dim), (parts,), jnp.float32, smallest / len(cuts), top_value / len(cuts))
        return jnp.repeat(jnp.exp(steps), dims[dim] // parts).reshape((-1,) + (1,) * (len(dims) - dim - 1))

    loudness = one(*cuts[0])
    for cut in cuts[1:]:
        loudness = loudness * one(*cut)
    return loudness


def bell_draw(stream_key, extent, scale, limit, pieces=(), kind=jnp.bfloat16):
    drawn = scale * jax.random.normal(stream_key, extent, jnp.float32)
    if pieces:
        drawn = drawn * steps_of(stream_key, extent, pieces, -0.22, 0.18)
    return jnp.clip(drawn, -limit, limit).astype(kind)


def setup_inputs(seed: int = 0) -> dict:
    keys = jax.random.split(jax.random.key(seed), 4)
    return {
        "tokens": bell_draw(keys[0], (ROWS, COLS, D), 1.0, 6.0, ((0, 8), (1, 32))),
        "qkv_weight": draw_qkv_weight(jax.random.fold_in(keys[3], 71), 0),
        "proj_weight": bell_draw(keys[2], (D, D), D ** -0.5, 0.1875),
    }


def layer_norm(values):
    mean = lax.optimization_barrier(jnp.mean(values, axis=-1, keepdims=True))
    centered = values - mean
    variance = lax.optimization_barrier(jnp.mean(centered * centered, axis=-1, keepdims=True))
    return centered * lax.rsqrt(variance + 1e-05)

def attend(queries, pairs, valid):
    groups = HEADS // 2
    query_groups = queries.reshape(-1, groups, 2 * HD).transpose(1, 0, 2)
    key_groups = pairs[:, :D].reshape(-1, groups, 2 * HD).transpose(1, 0, 2)
    value_groups = pairs[:, D:].reshape(-1, groups, 2 * HD).transpose(1, 0, 2)

    def one_group(items):
        query_part, key_part, value_part = items
        query_heads = query_part.reshape(-1, 2, HD).astype(jnp.float32)
        key_heads = key_part.reshape(-1, 2, HD).astype(jnp.float32)
        value_heads = value_part.reshape(-1, 2, HD).astype(jnp.float32)
        scores = jnp.einsum('qhd,khd->hqk', query_heads, key_heads) * HD ** (-0.5)
        scores = jnp.where(valid[None, None, :], scores, -1e+30)
        top = lax.optimization_barrier(jnp.max(scores, axis=-1, keepdims=True))
        expo = jnp.exp(scores - top)
        weights = (expo / lax.optimization_barrier(jnp.sum(expo, axis=-1, keepdims=True))).astype(jnp.bfloat16)
        context = jnp.einsum('hqk,khd->qhd', weights.astype(jnp.float32), value_heads)
        return context.reshape(-1, 2 * HD).astype(jnp.bfloat16)
    outputs = lax.map(one_group, (query_groups, key_groups, value_groups))
    return outputs.transpose(1, 0, 2).reshape(-1, D)

def reference(tokens, qkv_weight, proj_weight):
    normed = layer_norm(tokens.astype(jnp.float32)).astype(jnp.bfloat16)
    pairs = jnp.dot(normed.reshape(-1, D), qkv_weight[:, D:], preferred_element_type=jnp.float32)
    pairs = pairs.astype(jnp.bfloat16).reshape(ROWS, COLS, 2 * D)
    pairs = jnp.concatenate([pairs[:, COLS - HALO:], pairs, pairs[:, :HALO]], axis=1)
    zeros_rim = jnp.zeros((HALO, COLS + 2 * HALO, 2 * D), jnp.bfloat16)
    padded = jnp.concatenate([zeros_rim, pairs, zeros_rim], axis=0)
    zero = jnp.zeros((), jnp.int32)

    def one_tile(index):
        row_tile = (index // N_LON).astype(jnp.int32)
        col_tile = (index % N_LON).astype(jnp.int32)
        window = lax.dynamic_slice(padded, (row_tile * TH, col_tile * TW, zero), (TH + 2 * HALO, TW + 2 * HALO, 2 * D))
        own_norm = lax.dynamic_slice(normed, (row_tile * TH, col_tile * TW, zero), (TH, TW, D)).reshape(TH * TW, D)
        own_tokens = lax.dynamic_slice(tokens, (row_tile * TH, col_tile * TW, zero), (TH, TW, D)).reshape(TH * TW, D)
        queries = jnp.dot(own_norm, qkv_weight[:, :D], preferred_element_type=jnp.float32).astype(jnp.bfloat16)
        row_ids = row_tile * TH + jnp.arange(TH + 2 * HALO, dtype=jnp.int32) - HALO
        valid_rows = (row_ids >= 0) & (row_ids < ROWS)
        valid = jnp.repeat(valid_rows, TW + 2 * HALO)
        context = attend(queries, window.reshape(-1, 2 * D), valid)
        result = own_tokens.astype(jnp.float32) + jnp.dot(context, proj_weight, preferred_element_type=jnp.float32)
        return result.astype(jnp.bfloat16).reshape(TH, TW, D)
    tiles = lax.map(one_tile, jnp.arange(N_LAT * N_LON, dtype=jnp.int32))
    tiles = tiles.reshape(N_LAT, N_LON, TH, TW, D).transpose(0, 2, 1, 3, 4)
    return tiles.reshape(ROWS, COLS, D)
```

```python
import math

import jax
import jax.numpy as jnp
from jax import lax
from jax.experimental import pallas as pl
from jax.experimental.pallas import tpu as pltpu
from jax.sharding import PartitionSpec as P

D = 1024
HEADS = 16
TH = 40
TW = 24
HALO = 2
HD = 64
OWN = TH * TW
CORNER = 16
SIDE = TH * HALO
CAP = HALO * TW
RIM = 2 * SIDE + 2 * CAP + 4 * CORNER
KEYS = OWN + RIM
CHUNK = 256
PAIRS = HEADS // 2
SCALE = HD ** (-0.5) * math.log2(math.e)
SAFE = 100.0
MESH = pl.DeviceIdType.MESH
F32 = jnp.float32
BF16 = jnp.bfloat16

LEFT, RIGHT, TOP, BOTTOM = 0, SIDE, 2 * SIDE, 2 * SIDE + CAP
CORNERS = 2 * SIDE + 2 * CAP


def picked_rows():
    i = lax.broadcasted_iota(jnp.int32, (2 * SIDE + 4 * CORNER, OWN), 0)
    side = jnp.where(i >= SIDE, i - SIDE, i)
    side_row = (side // 2) * TW + side % 2 + jnp.where(i >= SIDE, TW - HALO, 0)
    j = i - 2 * SIDE
    which = j // CORNER
    c = j % 4
    corner_row = (
        (c // 2) * TW + c % 2 + (which % 2) * (TW - HALO) + (which // 2) * (OWN - CAP)
    )
    return jnp.where(i < 2 * SIDE, side_row, corner_row)


def rim_mask(lat, lats, shape):
    i = lax.broadcasted_iota(jnp.int32, shape, 0)
    corner = (i - CORNERS) // CORNER
    in_corner = i >= CORNERS
    upper = ((i >= TOP) & (i < BOTTOM)) | (in_corner & (corner < 2))
    lower = ((i >= BOTTOM) & (i < CORNERS)) | (in_corner & (corner >= 2))
    bad = in_corner & ((i - CORNERS) % CORNER >= 4)
    bad = bad | (upper & (lat == 0)) | (lower & (lat == lats - 1))
    return jnp.where(bad, 0.0, 1.0).astype(F32)


def project_kernel(lats, lons, tok_hbm, w_hbm, q_hbm, k_hbm, v_hbm, stat_ref,
                   tok, normed, w, edge, rim, qs, ks, vs,
                   tok_sem, w_sem, out_sem, send_sem, recv_sem):
    lat, lon = lax.axis_index("lat"), lax.axis_index("lon")
    up, down = lax.rem(lat + lats - 1, lats), lax.rem(lat + 1, lats)
    west, east = lax.rem(lon + lons - 1, lons), lax.rem(lon + 1, lons)
    barrier = pltpu.get_barrier_semaphore()
    around = [(lat, west), (lat, east), (up, lon), (down, lon),
              (up, west), (up, east), (down, west), (down, east)]
    for device in around:
        pl.semaphore_signal(barrier, inc=1, device_id=device, device_id_type=MESH)

    tok_copy = pltpu.make_async_copy(tok_hbm, tok, tok_sem)
    tok_copy.start()
    w_copies = []
    order = list(range(4, 12)) + list(range(4))
    for c in order:
        cols = pl.ds(c * CHUNK, CHUNK)
        copy = pltpu.make_async_copy(w_hbm.at[:, cols], w.at[c], w_sem.at[c])
        copy.start()
        w_copies.append(copy)
    tok_copy.wait()

    rows = 64
    for r in range(0, OWN, rows):
        x = tok[r:r + rows, :].astype(F32)
        centered = x - jnp.mean(x, axis=-1, keepdims=True)
        var = jnp.mean(centered * centered, axis=-1, keepdims=True)
        normed[r:r + rows, :] = (centered * lax.rsqrt(var + 1e-05)).astype(BF16)

    take = (picked_rows() == lax.broadcasted_iota(jnp.int32, (2 * SIDE + 4 * CORNER, OWN), 1))
    take = jnp.where(take, 1.0, 0.0).astype(BF16)
    edge[...] = jnp.dot(take, normed[...], preferred_element_type=F32).astype(BF16)

    pl.semaphore_wait(barrier, 8)
    e0 = 2 * SIDE
    plan = [
        (edge.at[pl.ds(0, SIDE)], RIGHT, SIDE),
        (edge.at[pl.ds(SIDE, SIDE)], LEFT, SIDE),
        (normed.at[pl.ds(0, CAP)], BOTTOM, CAP),
        (normed.at[pl.ds(OWN - CAP, CAP)], TOP, CAP),
        (edge.at[pl.ds(e0, CORNER)], CORNERS + 3 * CORNER, CORNER),
        (edge.at[pl.ds(e0 + CORNER, CORNER)], CORNERS + 2 * CORNER, CORNER),
        (edge.at[pl.ds(e0 + 2 * CORNER, CORNER)], CORNERS + CORNER, CORNER),
        (edge.at[pl.ds(e0 + 3 * CORNER, CORNER)], CORNERS, CORNER),
    ]
    sends = []
    for n, ((src, at, size), device) in enumerate(zip(plan, around)):
        copy = pltpu.make_async_remote_copy(
            src_ref=src, dst_ref=rim.at[pl.ds(at, size)],
            send_sem=send_sem.at[n], recv_sem=recv_sem.at[n],
            device_id=device, device_id_type=MESH)
        copy.start()
        sends.append(copy)

    def norms(x, row):
        for half in range(2):
            part = x[:, half * 128:half * 128 + 128]
            top = jnp.max(jnp.sum(part * part, axis=1, keepdims=True), axis=0, keepdims=True)
            stat_ref[row + half:row + half + 1, :] = jnp.broadcast_to(top, (1, 128))

    outs = []

    def put(src, dst):
        copy = pltpu.make_async_copy(src, dst, out_sem.at[len(outs)])
        copy.start()
        outs.append(copy)

    for n, c in enumerate(order):
        w_copies[n].wait()
        y = jnp.dot(normed[...], w[c], preferred_element_type=F32)
        cols = slice((c % 4) * CHUNK, (c % 4) * CHUNK + CHUNK)
        at = pl.ds((c % 4) * CHUNK, CHUNK)
        if c < 4:
            y = y * SCALE
            norms(y, 2 * c)
            qs[:, cols] = y.astype(BF16)
            put(qs.at[:, at], q_hbm.at[:, at])
        elif c < 8:
            norms(y, PAIRS + 2 * (c - 4))
            ks[0:OWN, cols] = y.astype(BF16)
            put(ks.at[pl.ds(0, OWN), at], k_hbm.at[pl.ds(0, OWN), at])
        else:
            vs[0:OWN, cols] = y.astype(BF16)
            put(vs.at[pl.ds(0, OWN), at], v_hbm.at[pl.ds(0, OWN), at])

    for copy in sends:
        copy.wait()

    c0 = CORNERS
    stand = normed[0:CAP, :]
    for lo, hi, at_end in ((TOP, BOTTOM, 0), (c0, c0 + 32, 0),
                           (BOTTOM, c0, lats - 1), (c0 + 32, c0 + 64, lats - 1)):
        rim[lo:hi, :] = jnp.where(lat == at_end, stand[0:hi - lo], rim[lo:hi, :])
    mask = rim_mask(lat, lats, (RIM, CHUNK))
    for c in range(4, 12):
        y = jnp.dot(rim[...], w[c], preferred_element_type=F32)
        cols = slice((c % 4) * CHUNK, (c % 4) * CHUNK + CHUNK)
        at = pl.ds((c % 4) * CHUNK, CHUNK)
        if c < 8:
            norms(y, 2 * PAIRS + 2 * (c - 4))
            ks[OWN:KEYS, cols] = y.astype(BF16)
            put(ks.at[pl.ds(OWN, RIM), at], k_hbm.at[pl.ds(OWN, RIM), at])
        else:
            vs[OWN:KEYS, cols] = (y * mask).astype(BF16)
            put(vs.at[pl.ds(OWN, RIM), at], v_hbm.at[pl.ds(OWN, RIM), at])
    for copy in outs:
        copy.wait()


def attend_kernel(lats, lat_ref, stat_ref, q_ref, k_ref, v_ref, tok_hbm, wp_hbm, out_hbm,
                  ones, ctx, tok, wp, out, tok_sem, wp_sem, out_sem):
    g = pl.program_id(0)
    tok_copy = pltpu.make_async_copy(tok_hbm, tok, tok_sem)
    wp_copy = pltpu.make_async_copy(wp_hbm, wp, wp_sem)

    @pl.when(g == 0)
    def _():
        tok_copy.start()
        wp_copy.start()
        ones[0:OWN, :] = jnp.ones((OWN, 128), BF16)
        ones[OWN:KEYS, :] = rim_mask(lat_ref[0], lats, (RIM, 128)).astype(BF16)

    rows = 240
    low = lax.broadcasted_iota(jnp.int32, (1, 128), 1) < HD

    def run(with_top):
        k = k_ref[...]
        v = v_ref[...]
        unit = ones[...]
        va = jnp.where(low, v, unit)
        vb = jnp.where(low, unit, v)
        for r in range(0, OWN, rows):
            q = q_ref[r:r + rows, :]
            zero = jnp.zeros_like(q)
            parts = []
            for h in range(2):
                qh = jnp.where(low, q, zero) if h == 0 else jnp.where(low, zero, q)
                s = lax.dot_general(qh, k, (((1,), (1,)), ((), ())), preferred_element_type=F32)
                if with_top:
                    s = s - jnp.max(s, axis=1, keepdims=True)
                p = jnp.exp2(s).astype(BF16)
                parts.append(jnp.dot(p, va if h == 0 else vb, preferred_element_type=F32))
            total = pltpu.roll(jnp.where(low, parts[1], parts[0]), HD, 1)
            done = jnp.where(low, parts[0], parts[1]) / total
            ctx[g, r:r + rows, :] = done.astype(BF16)

    k_top = jnp.maximum(stat_ref[PAIRS + g, 0], stat_ref[2 * PAIRS + g, 0])
    safe = stat_ref[g, 0] * k_top <= SAFE * SAFE

    @pl.when(safe)
    def _():
        run(False)

    @pl.when(jnp.logical_not(safe))
    def _():
        run(True)

    @pl.when(g == PAIRS - 1)
    def _():
        tok_copy.wait()
        wp_copy.wait()
        copies = []
        for n, r in enumerate(range(0, OWN, rows)):
            context = jnp.concatenate([ctx[p, r:r + rows, :] for p in range(PAIRS)], axis=1)
            y = jnp.dot(context, wp[...], preferred_element_type=F32)
            y = y + tok[r:r + rows, :].astype(F32)
            out[r:r + rows, :] = y.astype(BF16)
            part = pl.ds(r, rows)
            copy = pltpu.make_async_copy(out.at[part], out_hbm.at[part], out_sem.at[n])
            copy.start()
            copies.append(copy)
        for copy in copies:
            copy.wait()


def local(lats, lons, tokens, qkv_weight, proj_weight):
    flat = tokens.reshape(OWN, D)
    any_spec = pl.BlockSpec(memory_space=pl.ANY)
    vm = pltpu.VMEM
    dma = pltpu.SemaphoreType.DMA
    q, k, v, stat = pl.pallas_call(
        lambda *refs: project_kernel(lats, lons, *refs),
        out_shape=[
            jax.ShapeDtypeStruct((OWN, D), BF16),
            jax.ShapeDtypeStruct((KEYS, D), BF16),
            jax.ShapeDtypeStruct((KEYS, D), BF16),
            jax.ShapeDtypeStruct((3 * PAIRS, 128), F32),
        ],
        in_specs=[any_spec, any_spec],
        out_specs=[any_spec, any_spec, any_spec, pl.BlockSpec(memory_space=vm)],
        scratch_shapes=[
            vm((OWN, D), BF16), vm((OWN, D), BF16), vm((12, D, CHUNK), BF16),
            vm((2 * SIDE + 4 * CORNER, D), BF16), vm((RIM, D), BF16),
            vm((OWN, D), BF16), vm((KEYS, D), BF16), vm((KEYS, D), BF16),
            dma(()), dma((12,)), dma((20,)), dma((8,)), dma((8,)),
        ],
        compiler_params=pltpu.CompilerParams(
            collective_id=0, has_side_effects=True, vmem_limit_bytes=56 * 2 ** 20),
    )(flat, qkv_weight)
    lat = lax.axis_index("lat").astype(jnp.int32).reshape(1)
    smem = pl.BlockSpec(memory_space=pltpu.SMEM)
    mixed = pl.pallas_call(
        lambda *refs: attend_kernel(lats, *refs),
        grid=(PAIRS,),
        out_shape=jax.ShapeDtypeStruct((OWN, D), BF16),
        in_specs=[
            smem, smem,
            pl.BlockSpec((OWN, 128), lambda g: (0, g)),
            pl.BlockSpec((KEYS, 128), lambda g: (0, g)),
            pl.BlockSpec((KEYS, 128), lambda g: (0, g)),
            any_spec, any_spec,
        ],
        out_specs=any_spec,
        scratch_shapes=[
            vm((KEYS, 128), BF16), vm((PAIRS, OWN, 128), BF16), vm((OWN, D), BF16),
            vm((D, D), BF16), vm((OWN, D), BF16), dma(()), dma(()), dma((4,)),
        ],
        compiler_params=pltpu.CompilerParams(vmem_limit_bytes=56 * 2 ** 20),
    )(lat, stat, q, k, v, flat, proj_weight)
    return mixed.reshape(TH, TW, D)


def solution(mesh):
    lats, lons = mesh.shape["lat"], mesh.shape["lon"]
    return jax.shard_map(
        lambda *args: local(lats, lons, *args), mesh=mesh,
        in_specs=(P("lat", "lon", None), P(), P()), out_specs=P("lat", "lon", None),
        check_vma=False)
```

```python
import math

import jax
import jax.numpy as jnp
from jax import lax
from jax.experimental import pallas as pl
from jax.experimental.pallas import tpu as pltpu
from jax.sharding import PartitionSpec as P

D = 1024
HEADS = 16
TH = 40
TW = 24
HALO = 2
HD = 64
OWN = TH * TW
CORNER = 16
SIDE = TH * HALO
CAP = HALO * TW
RIM = 2 * SIDE + 2 * CAP + 4 * CORNER
KEYS = OWN + RIM
CHUNK = 512
CHUNKS = 3 * D // CHUNK
QS = D // CHUNK
PAIRS = HEADS // 2
SCALE = HD ** (-0.5) * math.log2(math.e)
SMALL = 2.0 ** -60
LARGE = 2.0 ** 100
MESH = pl.DeviceIdType.MESH
F32 = jnp.float32
BF16 = jnp.bfloat16

LEFT, RIGHT, TOP, BOTTOM = 0, SIDE, 2 * SIDE, 2 * SIDE + CAP
CORNERS = 2 * SIDE + 2 * CAP


def picked_rows():
    i = lax.broadcasted_iota(jnp.int32, (2 * SIDE + 4 * CORNER, OWN), 0)
    side = jnp.where(i >= SIDE, i - SIDE, i)
    side_row = (side // 2) * TW + side % 2 + jnp.where(i >= SIDE, TW - HALO, 0)
    j = i - 2 * SIDE
    which = j // CORNER
    c = j % 4
    corner_row = (
        (c // 2) * TW + c % 2 + (which % 2) * (TW - HALO) + (which // 2) * (OWN - CAP)
    )
    return jnp.where(i < 2 * SIDE, side_row, corner_row)


def rim_mask(lat, lats, shape):
    i = lax.broadcasted_iota(jnp.int32, shape, 0)
    corner = (i - CORNERS) // CORNER
    in_corner = i >= CORNERS
    upper = ((i >= TOP) & (i < BOTTOM)) | (in_corner & (corner < 2))
    lower = ((i >= BOTTOM) & (i < CORNERS)) | (in_corner & (corner >= 2))
    bad = in_corner & ((i - CORNERS) % CORNER >= 4)
    bad = bad | (upper & (lat == 0)) | (lower & (lat == lats - 1))
    return jnp.where(bad, 0.0, 1.0).astype(F32)


def project_kernel(lats, lons, tok_hbm, w_hbm, qkv_hbm,
                   tok, normed, w, edge, rim, res, res_rim,
                   tok_sem, w_sem, own_sem, rim_sem, send_sem, recv_sem):
    lat, lon = lax.axis_index("lat"), lax.axis_index("lon")
    up, down = lax.rem(lat + lats - 1, lats), lax.rem(lat + 1, lats)
    west, east = lax.rem(lon + lons - 1, lons), lax.rem(lon + 1, lons)
    barrier = pltpu.get_barrier_semaphore()
    around = [(lat, west), (lat, east), (up, lon), (down, lon),
              (up, west), (up, east), (down, west), (down, east)]
    for device in around:
        pl.semaphore_signal(barrier, inc=1, device_id=device, device_id_type=MESH)

    rows = 320

    def tok_copy(i):
        part = pl.ds(pl.multiple_of(i * rows, rows), rows)
        return pltpu.make_async_copy(tok_hbm.at[part], tok.at[part], tok_sem.at[i])

    for i in range(OWN // rows):
        tok_copy(i).start()

    def w_copy(c):
        at = pl.ds(pl.multiple_of(c * CHUNK, CHUNK), CHUNK)
        return pltpu.make_async_copy(w_hbm.at[:, at], w.at[c], w_sem.at[c])

    for c in range(CHUNKS):
        w_copy(c).start()

    def norm(i, carry):
        tok_copy(i).wait()
        part = pl.ds(pl.multiple_of(i * rows, rows), rows)
        x = tok[part, :].astype(F32)
        centered = x - jnp.mean(x, axis=-1, keepdims=True)
        var = jnp.mean(centered * centered, axis=-1, keepdims=True)
        normed[part, :] = (centered * lax.rsqrt(var + 1e-05)).astype(BF16)
        return carry

    lax.fori_loop(0, OWN // rows, norm, 0)

    take = (picked_rows() == lax.broadcasted_iota(jnp.int32, (2 * SIDE + 4 * CORNER, OWN), 1))
    take = jnp.where(take, 1.0, 0.0).astype(BF16)
    for c in range(2):
        cols = slice(c * 512, c * 512 + 512)
        edge[:, cols] = jnp.dot(take, normed[:, cols], preferred_element_type=F32).astype(BF16)

    pl.semaphore_wait(barrier, 8)
    e0 = 2 * SIDE
    plan = [
        (edge.at[pl.ds(0, SIDE)], RIGHT, SIDE),
        (edge.at[pl.ds(SIDE, SIDE)], LEFT, SIDE),
        (normed.at[pl.ds(0, CAP)], BOTTOM, CAP),
        (normed.at[pl.ds(OWN - CAP, CAP)], TOP, CAP),
        (edge.at[pl.ds(e0, CORNER)], CORNERS + 3 * CORNER, CORNER),
        (edge.at[pl.ds(e0 + CORNER, CORNER)], CORNERS + 2 * CORNER, CORNER),
        (edge.at[pl.ds(e0 + 2 * CORNER, CORNER)], CORNERS + CORNER, CORNER),
        (edge.at[pl.ds(e0 + 3 * CORNER, CORNER)], CORNERS, CORNER),
    ]
    sends = []
    for n, ((src, at, size), device) in enumerate(zip(plan, around)):
        copy = pltpu.make_async_remote_copy(
            src_ref=src, dst_ref=rim.at[pl.ds(at, size)],
            send_sem=send_sem.at[n], recv_sem=recv_sem.at[n],
            device_id=device, device_id_type=MESH)
        copy.start()
        sends.append(copy)

    def own_out(c):
        return pltpu.make_async_copy(
            res.at[c], qkv_hbm.at[c, pl.ds(0, OWN)], own_sem.at[c])

    def rim_out(c):
        return pltpu.make_async_copy(
            res_rim.at[c - QS], qkv_hbm.at[c, pl.ds(OWN, RIM)], rim_sem.at[c - QS])

    def own(c, carry):
        w_copy(c).wait()
        y = jnp.dot(normed[...], w[c], preferred_element_type=F32)
        y = y * jnp.where(c < QS, SCALE, 1.0)
        res[c] = y.astype(BF16)
        own_out(c).start()
        return carry

    lax.fori_loop(0, CHUNKS, own, 0)

    for copy in sends:
        copy.wait()

    c0 = CORNERS
    stand = normed[0:CAP, :]
    for lo, hi, at_end in ((TOP, BOTTOM, 0), (c0, c0 + 32, 0),
                           (BOTTOM, c0, lats - 1), (c0 + 32, c0 + 64, lats - 1)):
        rim[lo:hi, :] = jnp.where(lat == at_end, stand[0:hi - lo], rim[lo:hi, :])
    mask = rim_mask(lat, lats, (RIM, 128))
    mask = jnp.concatenate([mask] * (CHUNK // 128), axis=1)

    def outer(c, carry):
        y = jnp.dot(rim[...], w[c], preferred_element_type=F32)
        res_rim[c - QS] = (y * jnp.where(c < 2 * QS, 1.0, mask)).astype(BF16)
        rim_out(c).start()
        return carry

    lax.fori_loop(QS, CHUNKS, outer, 0)
    for c in range(CHUNKS):
        own_out(c).wait()
    for c in range(QS, CHUNKS):
        rim_out(c).wait()


def attend_kernel(lats, lat_ref, q_ref, k_ref, v_ref, tok_hbm, wp_hbm, out_hbm,
                  ones, ctx, tok, wp, out, tok_sem, wp_sem, out_sem):
    g = pl.program_id(0)
    tok_copy = pltpu.make_async_copy(tok_hbm, tok, tok_sem)
    wp_copy = pltpu.make_async_copy(wp_hbm, wp, wp_sem)

    @pl.when(g == 0)
    def _():
        tok_copy.start()
        wp_copy.start()
        ones[0:OWN, :] = jnp.ones((OWN, 128), BF16)
        ones[OWN:KEYS, :] = rim_mask(lat_ref[0], lats, (RIM, 128)).astype(BF16)

    rows = 240
    low = lax.broadcasted_iota(jnp.int32, (1, 128), 1) < HD

    def run(with_top):
        k = k_ref[0]
        v = v_ref[0]
        unit = ones[...]
        va = jnp.where(low, v, unit)
        vb = jnp.where(low, unit, v)
        fine = jnp.ones((8, 128), F32)
        for r in range(0, OWN, rows):
            q = q_ref[0, r:r + rows, :]
            zero = jnp.zeros_like(q)
            parts = []
            for h in range(2):
                qh = jnp.where(low, q, zero) if h == 0 else jnp.where(low, zero, q)
                s = lax.dot_general(qh, k, (((1,), (1,)), ((), ())), preferred_element_type=F32)
                if with_top:
                    s = s - jnp.max(s, axis=1, keepdims=True)
                p = jnp.exp2(s).astype(BF16)
                parts.append(jnp.dot(p, va if h == 0 else vb, preferred_element_type=F32))
            total = jnp.where(low, parts[1], parts[0])
            for i in range(0, rows, 8):
                t = total[i:i + 8, :]
                fine = jnp.where((t >= SMALL) & (t <= LARGE), fine, 0.0)
            done = jnp.where(low, parts[0], parts[1]) / pltpu.roll(total, HD, 1)
            ctx[g, r:r + rows, :] = done.astype(BF16)
        return jnp.min(fine) > 0.5

    safe = run(False)

    @pl.when(jnp.logical_not(safe))
    def _():
        run(True)

    @pl.when(g == PAIRS - 1)
    def _():
        tok_copy.wait()
        wp_copy.wait()
        copies = []
        for n, r in enumerate(range(0, OWN, rows)):
            context = jnp.concatenate([ctx[p, r:r + rows, :] for p in range(PAIRS)], axis=1)
            y = jnp.dot(context, wp[...], preferred_element_type=F32)
            y = y + tok[r:r + rows, :].astype(F32)
            out[r:r + rows, :] = y.astype(BF16)
            part = pl.ds(r, rows)
            copy = pltpu.make_async_copy(out.at[part], out_hbm.at[part], out_sem.at[n])
            copy.start()
            copies.append(copy)
        for copy in copies:
            copy.wait()


def local(lats, lons, tokens, qkv_weight, proj_weight):
    flat = tokens.reshape(OWN, D)
    any_spec = pl.BlockSpec(memory_space=pl.ANY)
    vm = pltpu.VMEM
    dma = pltpu.SemaphoreType.DMA
    qkv = pl.pallas_call(
        lambda *refs: project_kernel(lats, lons, *refs),
        out_shape=jax.ShapeDtypeStruct((CHUNKS, KEYS, CHUNK), BF16),
        in_specs=[any_spec, any_spec],
        out_specs=any_spec,
        scratch_shapes=[
            vm((OWN, D), BF16), vm((OWN, D), BF16), vm((CHUNKS, D, CHUNK), BF16),
            vm((2 * SIDE + 4 * CORNER, D), BF16), vm((RIM, D), BF16),
            vm((CHUNKS, OWN, CHUNK), BF16), vm((CHUNKS - QS, RIM, CHUNK), BF16),
            dma((OWN // 320,)), dma((CHUNKS,)), dma((CHUNKS,)), dma((CHUNKS - QS,)), dma((8,)), dma((8,)),
        ],
        compiler_params=pltpu.CompilerParams(
            collective_id=0, has_side_effects=True, vmem_limit_bytes=56 * 2 ** 20),
    )(flat, qkv_weight)
    lat = lax.axis_index("lat").astype(jnp.int32).reshape(1)
    smem = pl.BlockSpec(memory_space=pltpu.SMEM)
    per = CHUNK // 128
    mixed = pl.pallas_call(
        lambda *refs: attend_kernel(lats, *refs),
        grid=(PAIRS,),
        out_shape=jax.ShapeDtypeStruct((OWN, D), BF16),
        in_specs=[
            smem,
            pl.BlockSpec((1, OWN, 128), lambda g: (g // per, 0, g % per)),
            pl.BlockSpec((1, KEYS, 128), lambda g: (QS + g // per, 0, g % per)),
            pl.BlockSpec((1, KEYS, 128), lambda g: (2 * QS + g // per, 0, g % per)),
            any_spec, any_spec,
        ],
        out_specs=any_spec,
        scratch_shapes=[
            vm((KEYS, 128), BF16), vm((PAIRS, OWN, 128), BF16), vm((OWN, D), BF16),
            vm((D, D), BF16), vm((OWN, D), BF16), dma(()), dma(()), dma((4,)),
        ],
        compiler_params=pltpu.CompilerParams(vmem_limit_bytes=56 * 2 ** 20),
    )(lat, qkv, qkv, qkv, flat, proj_weight)
    return mixed.reshape(TH, TW, D)


def solution(mesh):
    lats, lons = mesh.shape["lat"], mesh.shape["lon"]
    return jax.shard_map(
        lambda *args: local(lats, lons, *args), mesh=mesh,
        in_specs=(P("lat", "lon", None), P(), P()), out_specs=P("lat", "lon", None),
        check_vma=False)
```

```python
import math

import jax
import jax.numpy as jnp
from jax import lax
from jax.experimental import pallas as pl
from jax.experimental.pallas import tpu as pltpu
from jax.sharding import PartitionSpec as P

D = 1024
HEADS = 16
TH = 40
TW = 24
HALO = 2
HD = 64
OWN = TH * TW
CORNER = 16
SIDE = TH * HALO
CAP = HALO * TW
RIM = 2 * SIDE + 2 * CAP + 4 * CORNER
KEYS = OWN + RIM
CHUNK = 1024
CHUNKS = 3 * D // CHUNK
QS = D // CHUNK
PAD = 1024
FIRST = 896
BLOCKS = ((0, 512), (512, FIRST))
COLS = 256
STEP = 4
PAIRS = HEADS // 2
SCALE = HD ** (-0.5) * math.log2(math.e)
SMALL = 2.0 ** -60
LARGE = 2.0 ** 100
MESH = pl.DeviceIdType.MESH
F32 = jnp.float32
BF16 = jnp.bfloat16

LEFT, RIGHT, TOP, BOTTOM = 0, SIDE, 2 * SIDE, 2 * SIDE + CAP
CORNERS = 2 * SIDE + 2 * CAP


def picked_rows():
    i = lax.broadcasted_iota(jnp.int32, (2 * SIDE + 4 * CORNER, OWN), 0)
    side = jnp.where(i >= SIDE, i - SIDE, i)
    side_row = (side // 2) * TW + side % 2 + jnp.where(i >= SIDE, TW - HALO, 0)
    j = i - 2 * SIDE
    which = j // CORNER
    c = j % 4
    corner_row = (
        (c // 2) * TW + c % 2 + (which % 2) * (TW - HALO) + (which // 2) * (OWN - CAP)
    )
    return jnp.where(i < 2 * SIDE, side_row, corner_row)


def rim_mask(lat, lats, first, shape, dim=0):
    i = lax.broadcasted_iota(jnp.int32, shape, dim) + (first - OWN)
    corner = (i - CORNERS) // CORNER
    in_corner = i >= CORNERS
    upper = ((i >= TOP) & (i < BOTTOM)) | (in_corner & (corner < 2))
    lower = ((i >= BOTTOM) & (i < CORNERS)) | (in_corner & (corner >= 2))
    bad = in_corner & ((i - CORNERS) % CORNER >= 4)
    bad = bad | (upper & (lat == 0)) | (lower & (lat == lats - 1))
    return jnp.where(bad, 0.0, 1.0).astype(F32)


def project_kernel(lats, lons, tok_hbm, w_hbm, qs, ks, vs,
                   tok, normed, w, edge, tok_sem, w_sem, send_sem, recv_sem):
    lat, lon = lax.axis_index("lat"), lax.axis_index("lon")
    up, down = lax.rem(lat + lats - 1, lats), lax.rem(lat + 1, lats)
    west, east = lax.rem(lon + lons - 1, lons), lax.rem(lon + 1, lons)
    barrier = pltpu.get_barrier_semaphore()
    around = [(lat, west), (lat, east), (up, lon), (down, lon),
              (up, west), (up, east), (down, west), (down, east)]
    for device in around:
        pl.semaphore_signal(barrier, inc=1, device_id=device, device_id_type=MESH)

    rows = 320

    def tok_copy(i):
        part = pl.ds(pl.multiple_of(i * rows, rows), rows)
        return pltpu.make_async_copy(tok_hbm.at[part], tok.at[part], tok_sem.at[i])

    for i in range(OWN // rows):
        tok_copy(i).start()

    def w_copy(c):
        at = pl.ds(pl.multiple_of(c * CHUNK, CHUNK), CHUNK)
        return pltpu.make_async_copy(w_hbm.at[:, at], w.at[c], w_sem.at[c])

    for c in range(CHUNKS):
        w_copy(c).start()

    def norm(i, carry):
        tok_copy(i).wait()
        part = pl.ds(pl.multiple_of(i * rows, rows), rows)
        x = tok[part, :].astype(F32)
        centered = x - jnp.mean(x, axis=-1, keepdims=True)
        var = jnp.mean(centered * centered, axis=-1, keepdims=True)
        normed[part, :] = (centered * lax.rsqrt(var + 1e-05)).astype(BF16)
        return carry

    lax.fori_loop(0, OWN // rows, norm, 0)

    take = (picked_rows() == lax.broadcasted_iota(jnp.int32, (2 * SIDE + 4 * CORNER, OWN), 1))
    take = jnp.where(take, 1.0, 0.0).astype(BF16)
    for c in range(2):
        cols = slice(c * 512, c * 512 + 512)
        edge[:, cols] = jnp.dot(take, normed[0:OWN, cols], preferred_element_type=F32).astype(BF16)

    pl.semaphore_wait(barrier, 8)
    e0 = 2 * SIDE
    plan = [
        (edge.at[pl.ds(0, SIDE)], RIGHT, SIDE),
        (edge.at[pl.ds(SIDE, SIDE)], LEFT, SIDE),
        (normed.at[pl.ds(0, CAP)], BOTTOM, CAP),
        (normed.at[pl.ds(OWN - CAP, CAP)], TOP, CAP),
        (edge.at[pl.ds(e0, CORNER)], CORNERS + 3 * CORNER, CORNER),
        (edge.at[pl.ds(e0 + CORNER, CORNER)], CORNERS + 2 * CORNER, CORNER),
        (edge.at[pl.ds(e0 + 2 * CORNER, CORNER)], CORNERS + CORNER, CORNER),
        (edge.at[pl.ds(e0 + 3 * CORNER, CORNER)], CORNERS, CORNER),
    ]
    sends = []
    for n, ((src, at, size), device) in enumerate(zip(plan, around)):
        copy = pltpu.make_async_remote_copy(
            src_ref=src, dst_ref=normed.at[pl.ds(OWN + at, size)],
            send_sem=send_sem.at[n], recv_sem=recv_sem.at[n],
            device_id=device, device_id_type=MESH)
        copy.start()
        sends.append(copy)

    def put_q(y, at):
        t = (y * SCALE).T.astype(BF16)
        for h in range(HEADS):
            low = h % 2 * HD
            qs[h, low:low + HD, at] = t[h * HD:h * HD + HD, :]

    def put_k(y, at):
        y = y.astype(BF16)
        for p in range(PAIRS):
            ks[p, at, :] = y[:, p * 128:p * 128 + 128]

    def put_v(y, at):
        t = y.T.astype(BF16)
        for h in range(HEADS):
            vs[h, 0:HD, at] = t[h * HD:h * HD + HD, :]

    for c, put in ((0, put_q), (1, put_k), (2, put_v)):
        w_copy(c).wait()
        for lo, hi in BLOCKS:
            put(jnp.dot(normed[lo:hi, :], w[c], preferred_element_type=F32), slice(lo, hi))

    unit = rim_mask(lat, lats, 0, (16, KEYS), 1).astype(BF16)
    for h in range(HEADS):
        other = (1 - h % 2) * HD
        qs[h, other:other + HD, :] = jnp.zeros((HD, PAD), BF16)
        vs[h, HD:HD + 16, :] = unit

    for copy in sends:
        copy.wait()

    c0 = CORNERS
    stand = normed[0:CAP, :]
    for lo, hi, at_end in ((TOP, BOTTOM, 0), (c0, c0 + 32, 0),
                           (BOTTOM, c0, lats - 1), (c0 + 32, c0 + 64, lats - 1)):
        at = slice(OWN + lo, OWN + hi)
        normed[at, :] = jnp.where(lat == at_end, stand[0:hi - lo], normed[at, :])
    mask = rim_mask(lat, lats, FIRST, (KEYS - FIRST, 128))
    mask = jnp.concatenate([mask] * (D // 128), axis=1)
    y = jnp.dot(normed[FIRST:KEYS, :], w[1], preferred_element_type=F32)
    put_k(y, slice(FIRST, KEYS))
    y = jnp.dot(normed[FIRST:KEYS, :], w[2], preferred_element_type=F32)
    put_v(y * mask, slice(FIRST, KEYS))
    y = jnp.dot(normed[FIRST:PAD, :], w[0], preferred_element_type=F32)
    put_q(y, slice(FIRST, PAD))


def attend_kernel(q_ref, k_ref, v_ref, tok_hbm, wp_hbm, out_hbm,
                  ctx, tok, wp, out, tok_sem, wp_sem, out_sem):
    tok_copy = pltpu.make_async_copy(tok_hbm, tok, tok_sem)
    wp_copy = pltpu.make_async_copy(wp_hbm, wp, wp_sem)
    tok_copy.start()
    wp_copy.start()

    def run(g, with_top):
        fine = jnp.ones((1, COLS), F32)
        units = [(c, h) for j in range(STEP) for c in range(0, PAD, COLS)
                 for h in range(2 * j, 2 * j + 2)]
        halves = {}

        def scores(c, h):
            return jnp.dot(k_ref[g * STEP + h // 2], q_ref[g * 2 * STEP + h, :, c:c + COLS],
                           preferred_element_type=F32)

        def weights(s):
            if with_top:
                s = s - jnp.max(s, axis=0, keepdims=True)
            return jnp.exp2(s).astype(BF16)

        def finish(c, h, p, fine):
            o = jnp.dot(v_ref[g * 2 * STEP + h], p, preferred_element_type=F32)
            total = o[HD:HD + 1, :]
            fine = jnp.where((total >= SMALL) & (total <= LARGE), fine, 0.0)
            halves[h] = o[0:HD, :] * (1.0 / total)
            if h % 2 == 1:
                pair = jnp.concatenate([halves[h - 1], halves[h]], axis=0)
                ctx[g * STEP + h // 2, c:c + COLS, :] = pair.T.astype(BF16)
            return fine

        s = scores(*units[0])
        held = None
        for n, unit in enumerate(units):
            later = scores(*units[n + 1]) if n + 1 < len(units) else None
            p = weights(s)
            if held is not None:
                fine = finish(*units[n - 1], held, fine)
            held, s = p, later
        return finish(*units[-1], held, fine)

    fine = lax.fori_loop(
        0, PAIRS // STEP, lambda g, fine: fine * run(g, False), jnp.ones((1, COLS), F32))

    @pl.when(jnp.logical_not(jnp.min(fine) > 0.5))
    def _():
        def again(g, carry):
            run(g, True)
            return carry

        lax.fori_loop(0, PAIRS // STEP, again, 0)

    tok_copy.wait()
    wp_copy.wait()
    rows = 240
    copies = []
    for n, r in enumerate(range(0, OWN, rows)):
        context = jnp.concatenate([ctx[p, r:r + rows, :] for p in range(PAIRS)], axis=1)
        y = jnp.dot(context, wp[...], preferred_element_type=F32)
        y = y + tok[r:r + rows, :].astype(F32)
        out[r:r + rows, :] = y.astype(BF16)
        part = pl.ds(r, rows)
        copy = pltpu.make_async_copy(out.at[part], out_hbm.at[part], out_sem.at[n])
        copy.start()
        copies.append(copy)
    for copy in copies:
        copy.wait()


def local(lats, lons, tokens, qkv_weight, proj_weight):
    flat = pltpu.with_memory_space_constraint(tokens.reshape(OWN, D), pltpu.HBM)
    any_spec = pl.BlockSpec(memory_space=pl.ANY)
    vm = pltpu.VMEM
    dma = pltpu.SemaphoreType.DMA
    in_vmem = pl.BlockSpec(memory_space=vm)
    q, k, v = pl.pallas_call(
        lambda *refs: project_kernel(lats, lons, *refs),
        out_shape=[
            vm((HEADS, 2 * HD, PAD), BF16), vm((PAIRS, KEYS, 128), BF16),
            vm((HEADS, HD + 16, KEYS), BF16),
        ],
        in_specs=[any_spec, any_spec],
        out_specs=[in_vmem] * 3,
        scratch_shapes=[
            vm((OWN, D), BF16), vm((KEYS, D), BF16), vm((CHUNKS, D, CHUNK), BF16),
            vm((2 * SIDE + 4 * CORNER, D), BF16),
            dma((OWN // 320,)), dma((CHUNKS,)), dma((8,)), dma((8,)),
        ],
        compiler_params=pltpu.CompilerParams(
            collective_id=0, has_side_effects=True, vmem_limit_bytes=40 * 2 ** 20),
    )(flat, qkv_weight)
    q, k, v = (pltpu.with_memory_space_constraint(x, vm) for x in (q, k, v))
    mixed = pl.pallas_call(
        attend_kernel,
        out_shape=jax.ShapeDtypeStruct((OWN, D), BF16),
        in_specs=[in_vmem] * 3 + [any_spec] * 2,
        out_specs=any_spec,
        scratch_shapes=[
            vm((PAIRS, PAD, 128), BF16), vm((OWN, D), BF16), vm((D, D), BF16),
            vm((OWN, D), BF16), dma(()), dma(()), dma((4,)),
        ],
        compiler_params=pltpu.CompilerParams(vmem_limit_bytes=40 * 2 ** 20),
    )(q, k, v, flat, proj_weight)
    return mixed.reshape(TH, TW, D)


def solution(mesh):
    lats, lons = mesh.shape["lat"], mesh.shape["lon"]
    return jax.shard_map(
        lambda *args: local(lats, lons, *args), mesh=mesh,
        in_specs=(P("lat", "lon", None), P(), P()), out_specs=P("lat", "lon", None),
        check_vma=False)
```

```python
import functools
import math

import jax
import jax.numpy as jnp
from jax import lax
from jax.experimental import pallas as pl
from jax.experimental.pallas import tpu as pltpu
from jax.sharding import PartitionSpec as P

D = 1024
HEADS = 16
TH = 40
TW = 24
HALO = 2
HD = 64
OWN = TH * TW
CORNER = 16
SIDE = TH * HALO
CAP = HALO * TW
RIM = 2 * SIDE + 2 * CAP + 4 * CORNER
KEYS = OWN + RIM
CHUNK = 1024
CHUNKS = 3 * D // CHUNK
QS = D // CHUNK
PAD = 1024
FIRST = 896
BLOCKS = ((0, 512), (512, FIRST))
Q_BLOCKS = ((0, 512), (512, OWN))
EARLY = 768
COLS = 256
STEP = 4
PAIRS = HEADS // 2
SCALE = HD ** (-0.5) * math.log2(math.e)
SMALL = 2.0 ** -60
LARGE = 2.0 ** 100
MESH = pl.DeviceIdType.MESH
F32 = jnp.float32
BF16 = jnp.bfloat16

LEFT, RIGHT, TOP, BOTTOM = 0, SIDE, 2 * SIDE, 2 * SIDE + CAP
CORNERS = 2 * SIDE + 2 * CAP


def picked_rows():
    i = lax.broadcasted_iota(jnp.int32, (2 * SIDE + 4 * CORNER, OWN), 0)
    side = jnp.where(i >= SIDE, i - SIDE, i)
    side_row = (side // 2) * TW + side % 2 + jnp.where(i >= SIDE, TW - HALO, 0)
    j = i - 2 * SIDE
    which = j // CORNER
    c = j % 4
    corner_row = (
        (c // 2) * TW + c % 2 + (which % 2) * (TW - HALO) + (which // 2) * (OWN - CAP)
    )
    return jnp.where(i < 2 * SIDE, side_row, corner_row)


def rim_mask(lat, lats, first, shape, dim=0):
    i = lax.broadcasted_iota(jnp.int32, shape, dim) + (first - OWN)
    corner = (i - CORNERS) // CORNER
    in_corner = i >= CORNERS
    upper = ((i >= TOP) & (i < BOTTOM)) | (in_corner & (corner < 2))
    lower = ((i >= BOTTOM) & (i < CORNERS)) | (in_corner & (corner >= 2))
    bad = in_corner & ((i - CORNERS) % CORNER >= 4)
    bad = bad | (upper & (lat == 0)) | (lower & (lat == lats - 1))
    return jnp.where(bad, 0.0, 1.0).astype(F32)


def attend(q_ref, k_ref, v_ref, g, step, keys, with_top, finish):
    units = [(c, h) for j in range(step) for c in range(0, PAD, COLS)
             for h in range(2 * j, 2 * j + 2)]

    def scores(c, h):
        return jnp.dot(k_ref[g * step + h // 2, keys, :], q_ref[g * 2 * step + h, :, c:c + COLS],
                       preferred_element_type=F32)

    def weights(s):
        if with_top:
            s = s - jnp.max(s, axis=0, keepdims=True)
        return jnp.exp2(s).astype(BF16)

    def context(unit, p):
        c, h = unit
        o = jnp.dot(v_ref[g * 2 * step + h, :, keys], p, preferred_element_type=F32)
        finish(g * 2 * step + h, g * step + h // 2, h % 2, slice(c, c + COLS), o)

    s = scores(*units[0])
    held = None
    for n, unit in enumerate(units):
        later = scores(*units[n + 1]) if n + 1 < len(units) else None
        p = weights(s)
        if held is not None:
            context(units[n - 1], held)
        held, s = p, later
    context(units[-1], held)


def project_kernel(lats, lons, tok_hbm, w_hbm, qs, ks, vs, early,
                   tok, normed, w, edge, tok_sem, w_sem, send_sem, recv_sem):
    lat, lon = lax.axis_index("lat"), lax.axis_index("lon")
    up, down = lax.rem(lat + lats - 1, lats), lax.rem(lat + 1, lats)
    west, east = lax.rem(lon + lons - 1, lons), lax.rem(lon + 1, lons)
    barrier = pltpu.get_barrier_semaphore()
    around = [(lat, west), (lat, east), (up, lon), (down, lon),
              (up, west), (up, east), (down, west), (down, east)]
    above, below = lat > 0, lat < lats - 1
    there = [None, None, above, below, above, above, below, below]
    behind = [None, None, below, above, below, below, above, above]

    def where_there(condition, action):
        if condition is None:
            action()
        else:
            pl.when(condition)(action)

    for device, condition in zip(around, there):
        where_there(condition, functools.partial(
            pl.semaphore_signal, barrier, inc=1, device_id=device, device_id_type=MESH))

    rows = 320

    def tok_copy(i):
        part = pl.ds(pl.multiple_of(i * rows, rows), rows)
        return pltpu.make_async_copy(tok_hbm.at[part], tok.at[part], tok_sem.at[i])

    for i in range(OWN // rows):
        tok_copy(i).start()

    def w_copy(c):
        at = pl.ds(pl.multiple_of(c * CHUNK, CHUNK), CHUNK)
        return pltpu.make_async_copy(w_hbm.at[:, at], w.at[c], w_sem.at[c])

    for c in range(CHUNKS):
        w_copy(c).start()

    def norm(i, carry):
        tok_copy(i).wait()
        part = pl.ds(pl.multiple_of(i * rows, rows), rows)
        x = tok[part, :].astype(F32)
        centered = x - jnp.mean(x, axis=-1, keepdims=True)
        var = jnp.mean(centered * centered, axis=-1, keepdims=True)
        normed[part, :] = (centered * lax.rsqrt(var + 1e-05)).astype(BF16)
        return carry

    lax.fori_loop(0, OWN // rows, norm, 0)

    take = (picked_rows() == lax.broadcasted_iota(jnp.int32, (2 * SIDE + 4 * CORNER, OWN), 1))
    take = jnp.where(take, 1.0, 0.0).astype(BF16)
    for c in range(2):
        cols = slice(c * 512, c * 512 + 512)
        edge[:, cols] = jnp.dot(take, normed[0:OWN, cols], preferred_element_type=F32).astype(BF16)

    pl.semaphore_wait(barrier, 2 + 3 * above.astype(jnp.int32) + 3 * below.astype(jnp.int32))
    e0 = 2 * SIDE
    plan = [
        (edge.at[pl.ds(0, SIDE)], RIGHT, SIDE),
        (edge.at[pl.ds(SIDE, SIDE)], LEFT, SIDE),
        (normed.at[pl.ds(0, CAP)], BOTTOM, CAP),
        (normed.at[pl.ds(OWN - CAP, CAP)], TOP, CAP),
        (edge.at[pl.ds(e0, CORNER)], CORNERS + 3 * CORNER, CORNER),
        (edge.at[pl.ds(e0 + CORNER, CORNER)], CORNERS + 2 * CORNER, CORNER),
        (edge.at[pl.ds(e0 + 2 * CORNER, CORNER)], CORNERS + CORNER, CORNER),
        (edge.at[pl.ds(e0 + 3 * CORNER, CORNER)], CORNERS, CORNER),
    ]
    sends = []
    for n, ((src, at, size), device) in enumerate(zip(plan, around)):
        copy = pltpu.make_async_remote_copy(
            src_ref=src, dst_ref=normed.at[pl.ds(OWN + at, size)],
            send_sem=send_sem.at[n], recv_sem=recv_sem.at[n],
            device_id=device, device_id_type=MESH)
        where_there(there[n], copy.start)
        sends.append(copy)

    def put_q(y, at):
        t = (y * SCALE).T.astype(BF16)
        for h in range(HEADS):
            low = h % 2 * HD
            qs[h, low:low + HD, at] = t[h * HD:h * HD + HD, :]

    def put_k(y, at):
        y = y.astype(BF16)
        for p in range(PAIRS):
            ks[p, at, :] = y[:, p * 128:p * 128 + 128]

    def put_v(y, at):
        t = y.T.astype(BF16)
        for h in range(HEADS):
            vs[h, 0:HD, at] = t[h * HD:h * HD + HD, :]

    for c, put, blocks in ((0, put_q, Q_BLOCKS), (1, put_k, BLOCKS), (2, put_v, BLOCKS)):
        w_copy(c).wait()
        for lo, hi in blocks:
            put(jnp.dot(normed[lo:hi, :], w[c], preferred_element_type=F32), slice(lo, hi))

    unit = rim_mask(lat, lats, 0, (16, KEYS), 1).astype(BF16)
    for h in range(HEADS):
        other = (1 - h % 2) * HD
        qs[h, other:other + HD, :] = jnp.zeros((HD, PAD), BF16)
        qs[h, h % 2 * HD:h % 2 * HD + HD, OWN:PAD] = jnp.zeros((HD, PAD - OWN), BF16)
        vs[h, HD:HD + 16, :] = unit

    def first_keys(g, carry):
        def finish(head, pair, odd, cols, o):
            early[head, :, cols] = o

        attend(qs, ks, vs, g, STEP, slice(0, EARLY), False, finish)
        return carry

    lax.fori_loop(0, PAIRS // STEP, first_keys, 0)

    for n, copy in enumerate(sends):
        where_there(there[n], copy.wait_send)
        where_there(behind[n], copy.wait_recv)

    c0 = CORNERS
    stand = normed[0:CAP, :]
    for lo, hi, at_end in ((TOP, BOTTOM, 0), (c0, c0 + 32, 0),
                           (BOTTOM, c0, lats - 1), (c0 + 32, c0 + 64, lats - 1)):
        def fill(lo=lo, hi=hi):
            normed[OWN + lo:OWN + hi, :] = stand[0:hi - lo]

        pl.when(lat == at_end)(fill)
    mask = rim_mask(lat, lats, FIRST, (KEYS - FIRST, 128))
    mask = jnp.concatenate([mask] * (D // 128), axis=1)
    y = jnp.dot(normed[FIRST:KEYS, :], w[1], preferred_element_type=F32)
    put_k(y, slice(FIRST, KEYS))
    y = jnp.dot(normed[FIRST:KEYS, :], w[2], preferred_element_type=F32)
    put_v(y * mask, slice(FIRST, KEYS))


def attend_kernel(q_ref, k_ref, v_ref, early, tok_hbm, wp_hbm, out_hbm,
                  ctx, tok, wp, out, tok_sem, wp_sem, out_sem):
    tok_copy = pltpu.make_async_copy(tok_hbm, tok, tok_sem)
    wp_copy = pltpu.make_async_copy(wp_hbm, wp, wp_sem)
    tok_copy.start()
    wp_copy.start()

    def run(g, step, with_top):
        state = [jnp.ones((1, COLS), F32), None]

        def finish(head, pair, odd, cols, o):
            if not with_top:
                o = o + early[head, :, cols]
            total = o[HD:HD + 1, :]
            state[0] = jnp.where((total >= SMALL) & (total <= LARGE), state[0], 0.0)
            half = o[0:HD, :] * (1.0 / total)
            if odd:
                ctx[pair, cols, :] = jnp.concatenate([state[1], half], axis=0).T.astype(BF16)
            state[1] = half

        keys = slice(0 if with_top else EARLY, KEYS)
        attend(q_ref, k_ref, v_ref, g, step, keys, with_top, finish)
        return state[0]

    fine = lax.fori_loop(
        0, PAIRS // STEP, lambda g, fine: fine * run(g, STEP, False), jnp.ones((1, COLS), F32))

    @pl.when(jnp.logical_not(jnp.min(fine) > 0.5))
    def _():
        def again(g, carry):
            run(g, 1, True)
            return carry

        lax.fori_loop(0, PAIRS, again, 0)

    tok_copy.wait()
    wp_copy.wait()
    rows = 240
    copies = []
    for n, r in enumerate(range(0, OWN, rows)):
        context = jnp.concatenate([ctx[p, r:r + rows, :] for p in range(PAIRS)], axis=1)
        y = jnp.dot(context, wp[...], preferred_element_type=F32)
        y = y + tok[r:r + rows, :].astype(F32)
        out[r:r + rows, :] = y.astype(BF16)
        part = pl.ds(r, rows)
        copy = pltpu.make_async_copy(out.at[part], out_hbm.at[part], out_sem.at[n])
        copy.start()
        copies.append(copy)
    for copy in copies:
        copy.wait()


def local(lats, lons, tokens, qkv_weight, proj_weight):
    flat = pltpu.with_memory_space_constraint(tokens.reshape(OWN, D), pltpu.HBM)
    any_spec = pl.BlockSpec(memory_space=pl.ANY)
    vm = pltpu.VMEM
    dma = pltpu.SemaphoreType.DMA
    in_vmem = pl.BlockSpec(memory_space=vm)
    results = pl.pallas_call(
        lambda *refs: project_kernel(lats, lons, *refs),
        out_shape=[
            vm((HEADS, 2 * HD, PAD), BF16), vm((PAIRS, KEYS, 128), BF16),
            vm((HEADS, HD + 16, KEYS), BF16), vm((HEADS, HD + 16, PAD), F32),
        ],
        in_specs=[any_spec, any_spec],
        out_specs=[in_vmem] * 4,
        scratch_shapes=[
            vm((OWN, D), BF16), vm((KEYS, D), BF16), vm((CHUNKS, D, CHUNK), BF16),
            vm((2 * SIDE + 4 * CORNER, D), BF16),
            dma((OWN // 320,)), dma((CHUNKS,)), dma((8,)), dma((8,)),
        ],
        compiler_params=pltpu.CompilerParams(
            collective_id=0, has_side_effects=True, vmem_limit_bytes=40 * 2 ** 20),
    )(flat, qkv_weight)
    results = [pltpu.with_memory_space_constraint(x, vm) for x in results]
    mixed = pl.pallas_call(
        attend_kernel,
        out_shape=jax.ShapeDtypeStruct((OWN, D), BF16),
        in_specs=[in_vmem] * 4 + [any_spec] * 2,
        out_specs=any_spec,
        scratch_shapes=[
            vm((PAIRS, PAD, 128), BF16), vm((OWN, D), BF16), vm((D, D), BF16),
            vm((OWN, D), BF16), dma(()), dma(()), dma((4,)),
        ],
        compiler_params=pltpu.CompilerParams(vmem_limit_bytes=40 * 2 ** 20),
    )(*results, flat, proj_weight)
    return mixed.reshape(TH, TW, D)


def solution(mesh):
    lats, lons = mesh.shape["lat"], mesh.shape["lon"]
    return jax.shard_map(
        lambda *args: local(lats, lons, *args), mesh=mesh,
        in_specs=(P("lat", "lon", None), P(), P()), out_specs=P("lat", "lon", None),
        check_vma=False)
```

```python
import functools
import math

import jax
import jax.numpy as jnp
from jax import lax
from jax.experimental import pallas as pl
from jax.experimental.pallas import tpu as pltpu
from jax.sharding import PartitionSpec as P

D = 1024
HEADS = 16
TH = 40
TW = 24
HALO = 2
HD = 64
OWN = TH * TW
CORNER = 16
SIDE = TH * HALO
CAP = HALO * TW
RIM = 2 * SIDE + 2 * CAP + 4 * CORNER
KEYS = OWN + RIM
CHUNK = 1024
CHUNKS = 3 * D // CHUNK
QS = D // CHUNK
PAD = 1024
FIRST = 896
BLOCKS = ((0, 512), (512, FIRST))
Q_BLOCKS = ((0, 512), (512, OWN))
EARLY = 768
COLS = 256
STEP = 4
PAIRS = HEADS // 2
SCALE = HD ** (-0.5) * math.log2(math.e)
SMALL = 2.0 ** -60
LARGE = 2.0 ** 100
MESH = pl.DeviceIdType.MESH
F32 = jnp.float32
BF16 = jnp.bfloat16

LEFT, RIGHT, TOP, BOTTOM = 0, SIDE, 2 * SIDE, 2 * SIDE + CAP
CORNERS = 2 * SIDE + 2 * CAP


def picked_rows():
    i = lax.broadcasted_iota(jnp.int32, (2 * SIDE + 4 * CORNER, OWN), 0)
    side = jnp.where(i >= SIDE, i - SIDE, i)
    side_row = (side // 2) * TW + side % 2 + jnp.where(i >= SIDE, TW - HALO, 0)
    j = i - 2 * SIDE
    which = j // CORNER
    c = j % 4
    corner_row = (
        (c // 2) * TW + c % 2 + (which % 2) * (TW - HALO) + (which // 2) * (OWN - CAP)
    )
    return jnp.where(i < 2 * SIDE, side_row, corner_row)


def rim_mask(lat, lats, first, shape, dim=0):
    i = lax.broadcasted_iota(jnp.int32, shape, dim) + (first - OWN)
    corner = (i - CORNERS) // CORNER
    in_corner = i >= CORNERS
    upper = ((i >= TOP) & (i < BOTTOM)) | (in_corner & (corner < 2))
    lower = ((i >= BOTTOM) & (i < CORNERS)) | (in_corner & (corner >= 2))
    bad = in_corner & ((i - CORNERS) % CORNER >= 4)
    bad = bad | (upper & (lat == 0)) | (lower & (lat == lats - 1))
    return jnp.where(bad, 0.0, 1.0).astype(F32)


def attend(q_ref, k_ref, v_ref, g, step, keys, with_top, finish):
    units = [(c, h) for j in range(step) for c in range(0, PAD, COLS)
             for h in range(2 * j, 2 * j + 2)]

    def scores(c, h):
        return jnp.dot(k_ref[g * step + h // 2, keys, :], q_ref[g * 2 * step + h, :, c:c + COLS],
                       preferred_element_type=F32)

    def weights(s):
        if with_top:
            s = s - jnp.max(s, axis=0, keepdims=True)
        return jnp.exp2(s).astype(BF16)

    def context(unit, p):
        c, h = unit
        o = jnp.dot(v_ref[g * 2 * step + h, :, keys], p, preferred_element_type=F32)
        finish(g * 2 * step + h, g * step + h // 2, h % 2, slice(c, c + COLS), o)

    s = scores(*units[0])
    held = None
    for n, unit in enumerate(units):
        later = scores(*units[n + 1]) if n + 1 < len(units) else None
        p = weights(s)
        if held is not None:
            context(units[n - 1], held)
        held, s = p, later
    context(units[-1], held)


def project_kernel(lats, lons, tok_hbm, w_hbm, qs, ks, vs, early,
                   tok, normed, w, edge, tok_sem, w_sem, send_sem, recv_sem):
    lat, lon = lax.axis_index("lat"), lax.axis_index("lon")
    up, down = lax.rem(lat + lats - 1, lats), lax.rem(lat + 1, lats)
    west, east = lax.rem(lon + lons - 1, lons), lax.rem(lon + 1, lons)
    barrier = pltpu.get_barrier_semaphore()
    around = [(lat, west), (lat, east), (up, lon), (down, lon),
              (up, west), (up, east), (down, west), (down, east)]
    above, below = lat > 0, lat < lats - 1
    there = [None, None, above, below, above, above, below, below]
    behind = [None, None, below, above, below, below, above, above]

    def where_there(condition, action):
        if condition is None:
            action()
        else:
            pl.when(condition)(action)

    for device, condition in zip(around, there):
        where_there(condition, functools.partial(
            pl.semaphore_signal, barrier, inc=1, device_id=device, device_id_type=MESH))

    rows = 320

    def tok_copy(i):
        part = pl.ds(pl.multiple_of(i * rows, rows), rows)
        return pltpu.make_async_copy(tok_hbm.at[part], tok.at[part], tok_sem.at[i])

    for i in range(OWN // rows):
        tok_copy(i).start()

    def w_copy(c):
        at = pl.ds(pl.multiple_of(c * CHUNK, CHUNK), CHUNK)
        return pltpu.make_async_copy(w_hbm.at[:, at], w.at[c], w_sem.at[c])

    for c in range(CHUNKS):
        w_copy(c).start()

    def norm(i, carry):
        tok_copy(i).wait()
        part = pl.ds(pl.multiple_of(i * rows, rows), rows)
        x = tok[part, :].astype(F32)
        centered = x - jnp.mean(x, axis=-1, keepdims=True)
        var = jnp.mean(centered * centered, axis=-1, keepdims=True)
        normed[part, :] = (centered * lax.rsqrt(var + 1e-05)).astype(BF16)
        return carry

    lax.fori_loop(0, OWN // rows, norm, 0)

    take = (picked_rows() == lax.broadcasted_iota(jnp.int32, (2 * SIDE + 4 * CORNER, OWN), 1))
    take = jnp.where(take, 1.0, 0.0).astype(BF16)
    for c in range(2):
        cols = slice(c * 512, c * 512 + 512)
        edge[:, cols] = jnp.dot(take, normed[0:OWN, cols], preferred_element_type=F32).astype(BF16)

    def put_q(y, at):
        t = (y * SCALE).T.astype(BF16)
        for h in range(HEADS):
            low = h % 2 * HD
            qs[h, low:low + HD, at] = t[h * HD:h * HD + HD, :]

    def put_k(y, at):
        y = y.astype(BF16)
        for p in range(PAIRS):
            ks[p, at, :] = y[:, p * 128:p * 128 + 128]

    def put_v(y, at):
        t = y.T.astype(BF16)
        for h in range(HEADS):
            vs[h, 0:HD, at] = t[h * HD:h * HD + HD, :]

    sends = []

    def send():
        pl.semaphore_wait(barrier, 2 + 3 * above.astype(jnp.int32) + 3 * below.astype(jnp.int32))
        e0 = 2 * SIDE
        plan = [
            (edge.at[pl.ds(0, SIDE)], RIGHT, SIDE),
            (edge.at[pl.ds(SIDE, SIDE)], LEFT, SIDE),
            (normed.at[pl.ds(0, CAP)], BOTTOM, CAP),
            (normed.at[pl.ds(OWN - CAP, CAP)], TOP, CAP),
            (edge.at[pl.ds(e0, CORNER)], CORNERS + 3 * CORNER, CORNER),
            (edge.at[pl.ds(e0 + CORNER, CORNER)], CORNERS + 2 * CORNER, CORNER),
            (edge.at[pl.ds(e0 + 2 * CORNER, CORNER)], CORNERS + CORNER, CORNER),
            (edge.at[pl.ds(e0 + 3 * CORNER, CORNER)], CORNERS, CORNER),
        ]
        for n, ((src, at, size), device) in enumerate(zip(plan, around)):
            copy = pltpu.make_async_remote_copy(
                src_ref=src, dst_ref=normed.at[pl.ds(OWN + at, size)],
                send_sem=send_sem.at[n], recv_sem=recv_sem.at[n],
                device_id=device, device_id_type=MESH)
            where_there(there[n], copy.start)
            sends.append(copy)

    for c, put, blocks in ((0, put_q, Q_BLOCKS), (1, put_k, BLOCKS), (2, put_v, BLOCKS)):
        if c == 2:
            send()
        w_copy(c).wait()
        for lo, hi in blocks:
            put(jnp.dot(normed[lo:hi, :], w[c], preferred_element_type=F32), slice(lo, hi))

    unit = rim_mask(lat, lats, 0, (16, KEYS), 1).astype(BF16)
    for h in range(HEADS):
        other = (1 - h % 2) * HD
        qs[h, other:other + HD, :] = jnp.zeros((HD, PAD), BF16)
        qs[h, h % 2 * HD:h % 2 * HD + HD, OWN:PAD] = jnp.zeros((HD, PAD - OWN), BF16)
        vs[h, HD:HD + 16, :] = unit

    def first_keys(g, carry):
        def finish(head, pair, odd, cols, o):
            early[head, :, cols] = o

        attend(qs, ks, vs, g, STEP, slice(0, EARLY), False, finish)
        return carry

    lax.fori_loop(0, PAIRS // STEP, first_keys, 0)

    for n, copy in enumerate(sends):
        where_there(there[n], copy.wait_send)
        where_there(behind[n], copy.wait_recv)

    c0 = CORNERS
    stand = normed[0:CAP, :]
    for lo, hi, at_end in ((TOP, BOTTOM, 0), (c0, c0 + 32, 0),
                           (BOTTOM, c0, lats - 1), (c0 + 32, c0 + 64, lats - 1)):
        def fill(lo=lo, hi=hi):
            normed[OWN + lo:OWN + hi, :] = stand[0:hi - lo]

        pl.when(lat == at_end)(fill)
    mask = rim_mask(lat, lats, FIRST, (KEYS - FIRST, 128))
    mask = jnp.concatenate([mask] * (D // 128), axis=1)
    y = jnp.dot(normed[FIRST:KEYS, :], w[1], preferred_element_type=F32)
    put_k(y, slice(FIRST, KEYS))
    y = jnp.dot(normed[FIRST:KEYS, :], w[2], preferred_element_type=F32)
    put_v(y * mask, slice(FIRST, KEYS))


def attend_kernel(q_ref, k_ref, v_ref, early, tok_hbm, wp_hbm, out_hbm,
                  ctx, tok, wp, out, tok_sem, wp_sem, out_sem):
    tok_copy = pltpu.make_async_copy(tok_hbm, tok, tok_sem)
    wp_copy = pltpu.make_async_copy(wp_hbm, wp, wp_sem)
    tok_copy.start()
    wp_copy.start()

    def run(g, step, with_top):
        state = [jnp.ones((1, COLS), F32), None]

        def finish(head, pair, odd, cols, o):
            if not with_top:
                o = o + early[head, :, cols]
            total = o[HD:HD + 1, :]
            state[0] = jnp.where((total >= SMALL) & (total <= LARGE), state[0], 0.0)
            half = o[0:HD, :] * (1.0 / total)
            if odd:
                ctx[pair, cols, :] = jnp.concatenate([state[1], half], axis=0).T.astype(BF16)
            state[1] = half

        keys = slice(0 if with_top else EARLY, KEYS)
        attend(q_ref, k_ref, v_ref, g, step, keys, with_top, finish)
        return state[0]

    fine = lax.fori_loop(
        0, PAIRS // STEP, lambda g, fine: fine * run(g, STEP, False), jnp.ones((1, COLS), F32))

    @pl.when(jnp.logical_not(jnp.min(fine) > 0.5))
    def _():
        def again(g, carry):
            run(g, 1, True)
            return carry

        lax.fori_loop(0, PAIRS, again, 0)

    tok_copy.wait()
    wp_copy.wait()
    rows = 240
    copies = []
    for n, r in enumerate(range(0, OWN, rows)):
        context = jnp.concatenate([ctx[p, r:r + rows, :] for p in range(PAIRS)], axis=1)
        y = jnp.dot(context, wp[...], preferred_element_type=F32)
        y = y + tok[r:r + rows, :].astype(F32)
        out[r:r + rows, :] = y.astype(BF16)
        part = pl.ds(r, rows)
        copy = pltpu.make_async_copy(out.at[part], out_hbm.at[part], out_sem.at[n])
        copy.start()
        copies.append(copy)
    for copy in copies:
        copy.wait()


def local(lats, lons, tokens, qkv_weight, proj_weight):
    flat = pltpu.with_memory_space_constraint(tokens.reshape(OWN, D), pltpu.HBM)
    any_spec = pl.BlockSpec(memory_space=pl.ANY)
    vm = pltpu.VMEM
    dma = pltpu.SemaphoreType.DMA
    in_vmem = pl.BlockSpec(memory_space=vm)
    results = pl.pallas_call(
        lambda *refs: project_kernel(lats, lons, *refs),
        out_shape=[
            vm((HEADS, 2 * HD, PAD), BF16), vm((PAIRS, KEYS, 128), BF16),
            vm((HEADS, HD + 16, KEYS), BF16), vm((HEADS, HD + 16, PAD), F32),
        ],
        in_specs=[any_spec, any_spec],
        out_specs=[in_vmem] * 4,
        scratch_shapes=[
            vm((OWN, D), BF16), vm((KEYS, D), BF16), vm((CHUNKS, D, CHUNK), BF16),
            vm((2 * SIDE + 4 * CORNER, D), BF16),
            dma((OWN // 320,)), dma((CHUNKS,)), dma((8,)), dma((8,)),
        ],
        compiler_params=pltpu.CompilerParams(
            collective_id=0, has_side_effects=True, vmem_limit_bytes=40 * 2 ** 20),
    )(flat, qkv_weight)
    results = [pltpu.with_memory_space_constraint(x, vm) for x in results]
    mixed = pl.pallas_call(
        attend_kernel,
        out_shape=jax.ShapeDtypeStruct((OWN, D), BF16),
        in_specs=[in_vmem] * 4 + [any_spec] * 2,
        out_specs=any_spec,
        scratch_shapes=[
            vm((PAIRS, PAD, 128), BF16), vm((OWN, D), BF16), vm((D, D), BF16),
            vm((OWN, D), BF16), dma(()), dma(()), dma((4,)),
        ],
        compiler_params=pltpu.CompilerParams(vmem_limit_bytes=40 * 2 ** 20),
    )(*results, flat, proj_weight)
    return mixed.reshape(TH, TW, D)


def solution(mesh):
    lats, lons = mesh.shape["lat"], mesh.shape["lon"]
    return jax.shard_map(
        lambda *args: local(lats, lons, *args), mesh=mesh,
        in_specs=(P("lat", "lon", None), P(), P()), out_specs=P("lat", "lon", None),
        check_vma=False)
```

```python
import functools
import math

import jax
import jax.numpy as jnp
from jax import lax
from jax.experimental import pallas as pl
from jax.experimental.pallas import tpu as pltpu
from jax.sharding import PartitionSpec as P

D = 1024
HEADS = 16
TH = 40
TW = 24
HALO = 2
HD = 64
OWN = TH * TW
CORNER = 16
SIDE = TH * HALO
CAP = HALO * TW
RIM = 2 * SIDE + 2 * CAP + 4 * CORNER
KEYS = OWN + RIM
CHUNK = 1024
CHUNKS = 3 * D // CHUNK
QS = D // CHUNK
PAD = 1024
FIRST = 896
BLOCKS = ((0, 512), (512, FIRST))
Q_BLOCKS = ((0, 512), (512, OWN))
EARLY = 768
COLS = 256
STEP = 4
PAIRS = HEADS // 2
SCALE = HD ** (-0.5) * math.log2(math.e)
SMALL = 2.0 ** -60
LARGE = 2.0 ** 100
MESH = pl.DeviceIdType.MESH
F32 = jnp.float32
BF16 = jnp.bfloat16

LEFT, RIGHT, TOP, BOTTOM = 0, SIDE, 2 * SIDE, 2 * SIDE + CAP
CORNERS = 2 * SIDE + 2 * CAP


def picked_rows():
    i = lax.broadcasted_iota(jnp.int32, (2 * SIDE + 4 * CORNER, 1), 0)
    side = jnp.where(i >= SIDE, i - SIDE, i)
    side_row = (side // 2) * TW + side % 2 + jnp.where(i >= SIDE, TW - HALO, 0)
    j = i - 2 * SIDE
    which = j // CORNER
    c = j % 4
    corner_row = (
        (c // 2) * TW + c % 2 + (which % 2) * (TW - HALO) + (which // 2) * (OWN - CAP)
    )
    return jnp.where(i < 2 * SIDE, side_row, corner_row)


def rim_mask(lat, lats, first, shape, dim=0):
    i = lax.broadcasted_iota(jnp.int32, shape, dim) + (first - OWN)
    corner = (i - CORNERS) // CORNER
    in_corner = i >= CORNERS
    upper = ((i >= TOP) & (i < BOTTOM)) | (in_corner & (corner < 2))
    lower = ((i >= BOTTOM) & (i < CORNERS)) | (in_corner & (corner >= 2))
    bad = in_corner & ((i - CORNERS) % CORNER >= 4)
    bad = bad | (upper & (lat == 0)) | (lower & (lat == lats - 1))
    return jnp.where(bad, 0.0, 1.0).astype(F32)


def attend(q_ref, k_ref, v_ref, g, step, keys, with_top, finish):
    units = [(c, h) for j in range(step) for c in range(0, PAD, COLS)
             for h in range(2 * j, 2 * j + 2)]

    def scores(c, h):
        return jnp.dot(k_ref[g * step + h // 2, keys, :], q_ref[g * 2 * step + h, :, c:c + COLS],
                       preferred_element_type=F32)

    def weights(s):
        if with_top:
            s = s - jnp.max(s, axis=0, keepdims=True)
        return jnp.exp2(s).astype(BF16)

    def context(unit, p):
        c, h = unit
        o = jnp.dot(v_ref[g * 2 * step + h, :, keys], p, preferred_element_type=F32)
        finish(g * 2 * step + h, g * step + h // 2, h % 2, slice(c, c + COLS), o)

    s = scores(*units[0])
    held = None
    for n, unit in enumerate(units):
        later = scores(*units[n + 1]) if n + 1 < len(units) else None
        p = weights(s)
        if held is not None:
            context(units[n - 1], held)
        held, s = p, later
    context(units[-1], held)


def project_kernel(lats, lons, tok_hbm, w_hbm, qs, ks, vs, early,
                   tok, normed, w, edge, tok_sem, w_sem, send_sem, recv_sem):
    lat, lon = lax.axis_index("lat"), lax.axis_index("lon")
    up, down = lax.rem(lat + lats - 1, lats), lax.rem(lat + 1, lats)
    west, east = lax.rem(lon + lons - 1, lons), lax.rem(lon + 1, lons)
    barrier = pltpu.get_barrier_semaphore()
    around = [(lat, west), (lat, east), (up, lon), (down, lon),
              (up, west), (up, east), (down, west), (down, east)]
    above, below = lat > 0, lat < lats - 1
    there = [None, None, above, below, above, above, below, below]
    behind = [None, None, below, above, below, below, above, above]

    def where_there(condition, action):
        if condition is None:
            action()
        else:
            pl.when(condition)(action)

    for device, condition in zip(around, there):
        where_there(condition, functools.partial(
            pl.semaphore_signal, barrier, inc=1, device_id=device, device_id_type=MESH))

    rows = 320

    def tok_copy(i):
        part = pl.ds(pl.multiple_of(i * rows, rows), rows)
        return pltpu.make_async_copy(tok_hbm.at[part], tok.at[part], tok_sem.at[i])

    for i in range(OWN // rows):
        tok_copy(i).start()

    def w_copy(c):
        at = pl.ds(pl.multiple_of(c * CHUNK, CHUNK), CHUNK)
        return pltpu.make_async_copy(w_hbm.at[:, at], w.at[c], w_sem.at[c])

    for c in range(CHUNKS):
        w_copy(c).start()

    unit = rim_mask(lat, lats, 0, (16, KEYS), 1).astype(BF16)
    for h in range(HEADS):
        other = (1 - h % 2) * HD
        qs[h, other:other + HD, :] = jnp.zeros((HD, PAD), BF16)
        qs[h, h % 2 * HD:h % 2 * HD + HD, OWN:PAD] = jnp.zeros((HD, PAD - OWN), BF16)
        vs[h, HD:HD + 16, :] = unit

    def norm(i, carry):
        tok_copy(i).wait()
        part = pl.ds(pl.multiple_of(i * rows, rows), rows)
        x = tok[part, :].astype(F32)
        centered = x - jnp.mean(x, axis=-1, keepdims=True)
        var = jnp.mean(centered * centered, axis=-1, keepdims=True)
        normed[part, :] = (centered * lax.rsqrt(var + 1e-05)).astype(BF16)
        return carry

    lax.fori_loop(0, OWN // rows, norm, 0)

    take = (picked_rows() == lax.broadcasted_iota(jnp.int32, (2 * SIDE + 4 * CORNER, OWN), 1))
    take = jnp.where(take, 1.0, 0.0).astype(BF16)
    for c in range(2):
        cols = slice(c * 512, c * 512 + 512)
        edge[:, cols] = jnp.dot(take, normed[0:OWN, cols], preferred_element_type=F32).astype(BF16)

    def put_q(y, at):
        t = (y * SCALE).T.astype(BF16)
        for h in range(HEADS):
            low = h % 2 * HD
            qs[h, low:low + HD, at] = t[h * HD:h * HD + HD, :]

    def put_k(y, at):
        y = y.astype(BF16)
        for p in range(PAIRS):
            ks[p, at, :] = y[:, p * 128:p * 128 + 128]

    def put_v(y, at):
        t = y.T.astype(BF16)
        for h in range(HEADS):
            vs[h, 0:HD, at] = t[h * HD:h * HD + HD, :]

    sends = []

    def send():
        pl.semaphore_wait(barrier, 2 + 3 * above.astype(jnp.int32) + 3 * below.astype(jnp.int32))
        e0 = 2 * SIDE
        plan = [
            (edge.at[pl.ds(0, SIDE)], RIGHT, SIDE),
            (edge.at[pl.ds(SIDE, SIDE)], LEFT, SIDE),
            (normed.at[pl.ds(0, CAP)], BOTTOM, CAP),
            (normed.at[pl.ds(OWN - CAP, CAP)], TOP, CAP),
            (edge.at[pl.ds(e0, CORNER)], CORNERS + 3 * CORNER, CORNER),
            (edge.at[pl.ds(e0 + CORNER, CORNER)], CORNERS + 2 * CORNER, CORNER),
            (edge.at[pl.ds(e0 + 2 * CORNER, CORNER)], CORNERS + CORNER, CORNER),
            (edge.at[pl.ds(e0 + 3 * CORNER, CORNER)], CORNERS, CORNER),
        ]
        for n, ((src, at, size), device) in enumerate(zip(plan, around)):
            copy = pltpu.make_async_remote_copy(
                src_ref=src, dst_ref=normed.at[pl.ds(OWN + at, size)],
                send_sem=send_sem.at[n], recv_sem=recv_sem.at[n],
                device_id=device, device_id_type=MESH)
            where_there(there[n], copy.start)
            sends.append(copy)

    for c, put, blocks in ((0, put_q, Q_BLOCKS), (1, put_k, BLOCKS), (2, put_v, BLOCKS)):
        if c == 2:
            send()
        w_copy(c).wait()
        for lo, hi in blocks:
            put(jnp.dot(normed[lo:hi, :], w[c], preferred_element_type=F32), slice(lo, hi))

    def first_keys(g, carry):
        def finish(head, pair, odd, cols, o):
            early[head, :, cols] = o

        attend(qs, ks, vs, g, STEP, slice(0, EARLY), False, finish)
        return carry

    lax.fori_loop(0, PAIRS // STEP, first_keys, 0)

    for n, copy in enumerate(sends):
        where_there(there[n], copy.wait_send)
        where_there(behind[n], copy.wait_recv)

    c0 = CORNERS
    stand = normed[0:CAP, :]
    for lo, hi, at_end in ((TOP, BOTTOM, 0), (c0, c0 + 32, 0),
                           (BOTTOM, c0, lats - 1), (c0 + 32, c0 + 64, lats - 1)):
        def fill(lo=lo, hi=hi):
            normed[OWN + lo:OWN + hi, :] = stand[0:hi - lo]

        pl.when(lat == at_end)(fill)
    mask = rim_mask(lat, lats, FIRST, (KEYS - FIRST, 128))
    mask = jnp.concatenate([mask] * (D // 128), axis=1)
    y = jnp.dot(normed[FIRST:KEYS, :], w[1], preferred_element_type=F32)
    put_k(y, slice(FIRST, KEYS))
    y = jnp.dot(normed[FIRST:KEYS, :], w[2], preferred_element_type=F32)
    put_v(y * mask, slice(FIRST, KEYS))


def attend_kernel(q_ref, k_ref, v_ref, early, tok_hbm, wp_hbm, out_hbm,
                  ctx, tok, wp, out, tok_sem, wp_sem, out_sem):
    tok_copy = pltpu.make_async_copy(tok_hbm, tok, tok_sem)
    wp_copy = pltpu.make_async_copy(wp_hbm, wp, wp_sem)
    tok_copy.start()
    wp_copy.start()

    def run(g, step, with_top):
        state = [jnp.ones((1, COLS), F32), None]

        def finish(head, pair, odd, cols, o):
            if not with_top:
                o = o + early[head, :, cols]
            total = o[HD:HD + 1, :]
            state[0] = jnp.where((total >= SMALL) & (total <= LARGE), state[0], 0.0)
            half = o[0:HD, :] * (1.0 / total)
            if odd:
                ctx[pair, cols, :] = jnp.concatenate([state[1], half], axis=0).T.astype(BF16)
            state[1] = half

        keys = slice(0 if with_top else EARLY, KEYS)
        attend(q_ref, k_ref, v_ref, g, step, keys, with_top, finish)
        return state[0]

    fine = lax.fori_loop(
        0, PAIRS // STEP, lambda g, fine: fine * run(g, STEP, False), jnp.ones((1, COLS), F32))

    @pl.when(jnp.logical_not(jnp.min(fine) > 0.5))
    def _():
        def again(g, carry):
            run(g, 1, True)
            return carry

        lax.fori_loop(0, PAIRS, again, 0)

    tok_copy.wait()
    wp_copy.wait()
    rows = 240
    copies = []
    for n, r in enumerate(range(0, OWN, rows)):
        context = jnp.concatenate([ctx[p, r:r + rows, :] for p in range(PAIRS)], axis=1)
        y = jnp.dot(context, wp[...], preferred_element_type=F32)
        y = y + tok[r:r + rows, :].astype(F32)
        out[r:r + rows, :] = y.astype(BF16)
        part = pl.ds(r, rows)
        copy = pltpu.make_async_copy(out.at[part], out_hbm.at[part], out_sem.at[n])
        copy.start()
        copies.append(copy)
    for copy in copies:
        copy.wait()


def local(lats, lons, tokens, qkv_weight, proj_weight):
    flat = pltpu.with_memory_space_constraint(tokens.reshape(OWN, D), pltpu.HBM)
    any_spec = pl.BlockSpec(memory_space=pl.ANY)
    vm = pltpu.VMEM
    dma = pltpu.SemaphoreType.DMA
    in_vmem = pl.BlockSpec(memory_space=vm)
    results = pl.pallas_call(
        lambda *refs: project_kernel(lats, lons, *refs),
        out_shape=[
            vm((HEADS, 2 * HD, PAD), BF16), vm((PAIRS, KEYS, 128), BF16),
            vm((HEADS, HD + 16, KEYS), BF16), vm((HEADS, HD + 16, PAD), F32),
        ],
        in_specs=[any_spec, any_spec],
        out_specs=[in_vmem] * 4,
        scratch_shapes=[
            vm((OWN, D), BF16), vm((KEYS, D), BF16), vm((CHUNKS, D, CHUNK), BF16),
            vm((2 * SIDE + 4 * CORNER, D), BF16),
            dma((OWN // 320,)), dma((CHUNKS,)), dma((8,)), dma((8,)),
        ],
        compiler_params=pltpu.CompilerParams(
            collective_id=0, has_side_effects=True, vmem_limit_bytes=40 * 2 ** 20),
    )(flat, qkv_weight)
    results = [pltpu.with_memory_space_constraint(x, vm) for x in results]
    mixed = pl.pallas_call(
        attend_kernel,
        out_shape=jax.ShapeDtypeStruct((OWN, D), BF16),
        in_specs=[in_vmem] * 4 + [any_spec] * 2,
        out_specs=any_spec,
        scratch_shapes=[
            vm((PAIRS, PAD, 128), BF16), vm((OWN, D), BF16), vm((D, D), BF16),
            vm((OWN, D), BF16), dma(()), dma(()), dma((4,)),
        ],
        compiler_params=pltpu.CompilerParams(vmem_limit_bytes=40 * 2 ** 20),
    )(*results, flat, proj_weight)
    return mixed.reshape(TH, TW, D)


def solution(mesh):
    lats, lons = mesh.shape["lat"], mesh.shape["lon"]
    return jax.shard_map(
        lambda *args: local(lats, lons, *args), mesh=mesh,
        in_specs=(P("lat", "lon", None), P(), P()), out_specs=P("lat", "lon", None),
        check_vma=False)
```

```python
import functools
import math

import jax
import jax.numpy as jnp
from jax import lax
from jax.experimental import pallas as pl
from jax.experimental.pallas import tpu as pltpu
from jax.sharding import PartitionSpec as P

D = 1024
HEADS = 16
TH = 40
TW = 24
HALO = 2
HD = 64
OWN = TH * TW
CORNER = 16
SIDE = TH * HALO
CAP = HALO * TW
RIM = 2 * SIDE + 2 * CAP + 4 * CORNER
KEYS = OWN + RIM
CHUNK = 1024
CHUNKS = 3 * D // CHUNK
QS = D // CHUNK
PAD = 1024
FIRST = 896
BLOCKS = ((0, 512), (512, FIRST))
Q_BLOCKS = ((0, 512), (512, OWN))
EARLY = 768
COLS = 256
STEP = 4
PAIRS = HEADS // 2
SCALE = HD ** (-0.5) * math.log2(math.e)
SMALL = 2.0 ** -60
LARGE = 2.0 ** 100
MESH = pl.DeviceIdType.MESH
F32 = jnp.float32
BF16 = jnp.bfloat16

LEFT, RIGHT, TOP, BOTTOM = 0, SIDE, 2 * SIDE, 2 * SIDE + CAP
CORNERS = 2 * SIDE + 2 * CAP


def picked_rows():
    i = lax.broadcasted_iota(jnp.int32, (2 * SIDE + 4 * CORNER, 1), 0)
    side = jnp.where(i >= SIDE, i - SIDE, i)
    side_row = (side // 2) * TW + side % 2 + jnp.where(i >= SIDE, TW - HALO, 0)
    j = i - 2 * SIDE
    which = j // CORNER
    c = j % 4
    corner_row = (
        (c // 2) * TW + c % 2 + (which % 2) * (TW - HALO) + (which // 2) * (OWN - CAP)
    )
    return jnp.where(i < 2 * SIDE, side_row, corner_row)


def rim_mask(lat, lats, first, shape, dim=0):
    i = lax.broadcasted_iota(jnp.int32, shape, dim) + (first - OWN)
    corner = (i - CORNERS) // CORNER
    in_corner = i >= CORNERS
    upper = ((i >= TOP) & (i < BOTTOM)) | (in_corner & (corner < 2))
    lower = ((i >= BOTTOM) & (i < CORNERS)) | (in_corner & (corner >= 2))
    bad = in_corner & ((i - CORNERS) % CORNER >= 4)
    bad = bad | (upper & (lat == 0)) | (lower & (lat == lats - 1))
    return jnp.where(bad, 0.0, 1.0).astype(F32)


def attend(q_ref, k_ref, v_ref, g, step, keys, with_top, finish):
    units = [(c, h) for j in range(step) for c in range(0, PAD, COLS)
             for h in range(2 * j, 2 * j + 2)]

    def scores(c, h):
        return jnp.dot(k_ref[g * step + h // 2, keys, :], q_ref[g * 2 * step + h, :, c:c + COLS],
                       preferred_element_type=F32)

    def weights(s):
        if with_top:
            s = s - jnp.max(s, axis=0, keepdims=True)
        return jnp.exp2(s).astype(BF16)

    def context(unit, p):
        c, h = unit
        o = jnp.dot(v_ref[g * 2 * step + h, :, keys], p, preferred_element_type=F32)
        finish(g * 2 * step + h, g * step + h // 2, h % 2, slice(c, c + COLS), o)

    s = scores(*units[0])
    held = None
    for n, unit in enumerate(units):
        later = scores(*units[n + 1]) if n + 1 < len(units) else None
        p = weights(s)
        if held is not None:
            context(units[n - 1], held)
        held, s = p, later
    context(units[-1], held)


def project_kernel(lats, lons, tok_hbm, w_hbm, qs, ks, vs, early,
                   tok, normed, w, edge, tok_sem, w_sem, send_sem, recv_sem):
    lat, lon = lax.axis_index("lat"), lax.axis_index("lon")
    up, down = lax.rem(lat + lats - 1, lats), lax.rem(lat + 1, lats)
    west, east = lax.rem(lon + lons - 1, lons), lax.rem(lon + 1, lons)
    barrier = pltpu.get_barrier_semaphore()
    around = [(lat, west), (lat, east), (up, lon), (down, lon),
              (up, west), (up, east), (down, west), (down, east)]
    above, below = lat > 0, lat < lats - 1
    there = [None, None, above, below, above, above, below, below]
    behind = [None, None, below, above, below, below, above, above]

    def where_there(condition, action):
        if condition is None:
            action()
        else:
            pl.when(condition)(action)

    for device, condition in zip(around, there):
        where_there(condition, functools.partial(
            pl.semaphore_signal, barrier, inc=1, device_id=device, device_id_type=MESH))

    rows = 320

    def tok_copy(i):
        part = pl.ds(pl.multiple_of(i * rows, rows), rows)
        return pltpu.make_async_copy(tok_hbm.at[part], tok.at[part], tok_sem.at[i])

    for i in range(OWN // rows):
        tok_copy(i).start()

    def w_copy(c):
        at = pl.ds(pl.multiple_of(c * CHUNK, CHUNK), CHUNK)
        return pltpu.make_async_copy(w_hbm.at[:, at], w.at[c], w_sem.at[c])

    for c in range(CHUNKS):
        w_copy(c).start()

    unit = rim_mask(lat, lats, 0, (16, KEYS), 1).astype(BF16)
    for h in range(HEADS):
        other = (1 - h % 2) * HD
        qs[h, other:other + HD, :] = jnp.zeros((HD, PAD), BF16)
        qs[h, h % 2 * HD:h % 2 * HD + HD, OWN:PAD] = jnp.zeros((HD, PAD - OWN), BF16)
        vs[h, HD:HD + 16, :] = unit

    def norm(i, carry):
        tok_copy(i).wait()
        part = pl.ds(pl.multiple_of(i * rows, rows), rows)
        x = tok[part, :].astype(F32)
        centered = x - jnp.mean(x, axis=-1, keepdims=True)
        var = jnp.mean(centered * centered, axis=-1, keepdims=True)
        normed[part, :] = (centered * lax.rsqrt(var + 1e-05)).astype(BF16)
        return carry

    lax.fori_loop(0, OWN // rows, norm, 0)

    take = (picked_rows() == lax.broadcasted_iota(jnp.int32, (2 * SIDE + 4 * CORNER, OWN), 1))
    take = jnp.where(take, 1.0, 0.0).astype(BF16)
    for c in range(2):
        cols = slice(c * 512, c * 512 + 512)
        edge[:, cols] = jnp.dot(take, normed[0:OWN, cols], preferred_element_type=F32).astype(BF16)

    def put_q(y, at):
        t = (y * SCALE).T.astype(BF16)
        for h in range(HEADS):
            low = h % 2 * HD
            qs[h, low:low + HD, at] = t[h * HD:h * HD + HD, :]

    def put_k(y, at):
        y = y.astype(BF16)
        for p in range(PAIRS):
            ks[p, at, :] = y[:, p * 128:p * 128 + 128]

    def put_v(y, at):
        t = y.T.astype(BF16)
        for h in range(HEADS):
            vs[h, 0:HD, at] = t[h * HD:h * HD + HD, :]

    sends = []

    def send():
        pl.semaphore_wait(barrier, 2 + 3 * above.astype(jnp.int32) + 3 * below.astype(jnp.int32))
        e0 = 2 * SIDE
        plan = [
            (edge.at[pl.ds(0, SIDE)], RIGHT, SIDE),
            (edge.at[pl.ds(SIDE, SIDE)], LEFT, SIDE),
            (normed.at[pl.ds(0, CAP)], BOTTOM, CAP),
            (normed.at[pl.ds(OWN - CAP, CAP)], TOP, CAP),
            (edge.at[pl.ds(e0, CORNER)], CORNERS + 3 * CORNER, CORNER),
            (edge.at[pl.ds(e0 + CORNER, CORNER)], CORNERS + 2 * CORNER, CORNER),
            (edge.at[pl.ds(e0 + 2 * CORNER, CORNER)], CORNERS + CORNER, CORNER),
            (edge.at[pl.ds(e0 + 3 * CORNER, CORNER)], CORNERS, CORNER),
        ]
        for n, ((src, at, size), device) in enumerate(zip(plan, around)):
            copy = pltpu.make_async_remote_copy(
                src_ref=src, dst_ref=normed.at[pl.ds(OWN + at, size)],
                send_sem=send_sem.at[n], recv_sem=recv_sem.at[n],
                device_id=device, device_id_type=MESH)
            where_there(there[n], copy.start)
            sends.append(copy)

    for c, put, blocks in ((0, put_q, Q_BLOCKS), (1, put_k, BLOCKS), (2, put_v, BLOCKS)):
        w_copy(c).wait()
        for lo, hi in blocks:
            put(jnp.dot(normed[lo:hi, :], w[c], preferred_element_type=F32), slice(lo, hi))
            if c == 2 and lo == 0:
                send()

    def first_keys(g, carry):
        def finish(head, pair, odd, cols, o):
            early[head, :, cols] = o

        attend(qs, ks, vs, g, STEP, slice(0, EARLY), False, finish)
        return carry

    lax.fori_loop(0, PAIRS // STEP, first_keys, 0)

    for n, copy in enumerate(sends):
        where_there(there[n], copy.wait_send)
        where_there(behind[n], copy.wait_recv)

    c0 = CORNERS
    stand = normed[0:CAP, :]
    for lo, hi, at_end in ((TOP, BOTTOM, 0), (c0, c0 + 32, 0),
                           (BOTTOM, c0, lats - 1), (c0 + 32, c0 + 64, lats - 1)):
        def fill(lo=lo, hi=hi):
            normed[OWN + lo:OWN + hi, :] = stand[0:hi - lo]

        pl.when(lat == at_end)(fill)
    mask = rim_mask(lat, lats, FIRST, (KEYS - FIRST, 128))
    mask = jnp.concatenate([mask] * (D // 128), axis=1)
    y = jnp.dot(normed[FIRST:KEYS, :], w[1], preferred_element_type=F32)
    put_k(y, slice(FIRST, KEYS))
    y = jnp.dot(normed[FIRST:KEYS, :], w[2], preferred_element_type=F32)
    put_v(y * mask, slice(FIRST, KEYS))


def attend_kernel(q_ref, k_ref, v_ref, early, tok_hbm, wp_hbm, out_hbm,
                  ctx, tok, wp, out, tok_sem, wp_sem, out_sem):
    tok_copy = pltpu.make_async_copy(tok_hbm, tok, tok_sem)
    wp_copy = pltpu.make_async_copy(wp_hbm, wp, wp_sem)
    tok_copy.start()
    wp_copy.start()

    def run(g, step, with_top):
        state = [jnp.ones((1, COLS), F32), None]

        def finish(head, pair, odd, cols, o):
            if not with_top:
                o = o + early[head, :, cols]
            total = o[HD:HD + 1, :]
            state[0] = jnp.where((total >= SMALL) & (total <= LARGE), state[0], 0.0)
            half = o[0:HD, :] * (1.0 / total)
            if odd:
                ctx[pair, cols, :] = jnp.concatenate([state[1], half], axis=0).T.astype(BF16)
            state[1] = half

        keys = slice(0 if with_top else EARLY, KEYS)
        attend(q_ref, k_ref, v_ref, g, step, keys, with_top, finish)
        return state[0]

    fine = lax.fori_loop(
        0, PAIRS // STEP, lambda g, fine: fine * run(g, STEP, False), jnp.ones((1, COLS), F32))

    @pl.when(jnp.logical_not(jnp.min(fine) > 0.5))
    def _():
        def again(g, carry):
            run(g, 1, True)
            return carry

        lax.fori_loop(0, PAIRS, again, 0)

    tok_copy.wait()
    wp_copy.wait()
    rows = 240
    copies = []
    for n, r in enumerate(range(0, OWN, rows)):
        context = jnp.concatenate([ctx[p, r:r + rows, :] for p in range(PAIRS)], axis=1)
        y = jnp.dot(context, wp[...], preferred_element_type=F32)
        y = y + tok[r:r + rows, :].astype(F32)
        out[r:r + rows, :] = y.astype(BF16)
        part = pl.ds(r, rows)
        copy = pltpu.make_async_copy(out.at[part], out_hbm.at[part], out_sem.at[n])
        copy.start()
        copies.append(copy)
    for copy in copies:
        copy.wait()


def local(lats, lons, tokens, qkv_weight, proj_weight):
    flat = pltpu.with_memory_space_constraint(tokens.reshape(OWN, D), pltpu.HBM)
    any_spec = pl.BlockSpec(memory_space=pl.ANY)
    vm = pltpu.VMEM
    dma = pltpu.SemaphoreType.DMA
    in_vmem = pl.BlockSpec(memory_space=vm)
    results = pl.pallas_call(
        lambda *refs: project_kernel(lats, lons, *refs),
        out_shape=[
            vm((HEADS, 2 * HD, PAD), BF16), vm((PAIRS, KEYS, 128), BF16),
            vm((HEADS, HD + 16, KEYS), BF16), vm((HEADS, HD + 16, PAD), F32),
        ],
        in_specs=[any_spec, any_spec],
        out_specs=[in_vmem] * 4,
        scratch_shapes=[
            vm((OWN, D), BF16), vm((KEYS, D), BF16), vm((CHUNKS, D, CHUNK), BF16),
            vm((2 * SIDE + 4 * CORNER, D), BF16),
            dma((OWN // 320,)), dma((CHUNKS,)), dma((8,)), dma((8,)),
        ],
        compiler_params=pltpu.CompilerParams(
            collective_id=0, has_side_effects=True, vmem_limit_bytes=40 * 2 ** 20),
    )(flat, qkv_weight)
    results = [pltpu.with_memory_space_constraint(x, vm) for x in results]
    mixed = pl.pallas_call(
        attend_kernel,
        out_shape=jax.ShapeDtypeStruct((OWN, D), BF16),
        in_specs=[in_vmem] * 4 + [any_spec] * 2,
        out_specs=any_spec,
        scratch_shapes=[
            vm((PAIRS, PAD, 128), BF16), vm((OWN, D), BF16), vm((D, D), BF16),
            vm((OWN, D), BF16), dma(()), dma(()), dma((4,)),
        ],
        compiler_params=pltpu.CompilerParams(vmem_limit_bytes=40 * 2 ** 20),
    )(*results, flat, proj_weight)
    return mixed.reshape(TH, TW, D)


def solution(mesh):
    lats, lons = mesh.shape["lat"], mesh.shape["lon"]
    return jax.shard_map(
        lambda *args: local(lats, lons, *args), mesh=mesh,
        in_specs=(P("lat", "lon", None), P(), P()), out_specs=P("lat", "lon", None),
        check_vma=False)
```

```python
import functools
import math

import jax
import jax.numpy as jnp
from jax import lax
from jax.experimental import pallas as pl
from jax.experimental.pallas import tpu as pltpu
from jax.sharding import PartitionSpec as P

D = 1024
HEADS = 16
TH = 40
TW = 24
HALO = 2
HD = 64
OWN = TH * TW
CORNER = 16
SIDE = TH * HALO
CAP = HALO * TW
RIM = 2 * SIDE + 2 * CAP + 4 * CORNER
KEYS = OWN + RIM
CHUNK = 1024
CHUNKS = 3 * D // CHUNK
QS = D // CHUNK
PAD = 1024
FIRST = 896
BLOCKS = ((0, 512), (512, FIRST))
Q_BLOCKS = ((0, 512), (512, OWN))
EARLY = 768
COLS = 256
STEP = 4
PAIRS = HEADS // 2
SCALE = HD ** (-0.5) * math.log2(math.e)
SMALL = 2.0 ** -60
LARGE = 2.0 ** 100
MESH = pl.DeviceIdType.MESH
F32 = jnp.float32
BF16 = jnp.bfloat16

LEFT, RIGHT, TOP, BOTTOM = 0, SIDE, 2 * SIDE, 2 * SIDE + CAP
CORNERS = 2 * SIDE + 2 * CAP


def picked_rows():
    i = lax.broadcasted_iota(jnp.int32, (2 * SIDE + 4 * CORNER, 1), 0)
    side = jnp.where(i >= SIDE, i - SIDE, i)
    side_row = (side // 2) * TW + side % 2 + jnp.where(i >= SIDE, TW - HALO, 0)
    j = i - 2 * SIDE
    which = j // CORNER
    c = j % 4
    corner_row = (
        (c // 2) * TW + c % 2 + (which % 2) * (TW - HALO) + (which // 2) * (OWN - CAP)
    )
    return jnp.where(i < 2 * SIDE, side_row, corner_row)


def rim_mask(lat, lats, first, shape, dim=0):
    i = lax.broadcasted_iota(jnp.int32, shape, dim) + (first - OWN)
    corner = (i - CORNERS) // CORNER
    in_corner = i >= CORNERS
    upper = ((i >= TOP) & (i < BOTTOM)) | (in_corner & (corner < 2))
    lower = ((i >= BOTTOM) & (i < CORNERS)) | (in_corner & (corner >= 2))
    bad = in_corner & ((i - CORNERS) % CORNER >= 4)
    bad = bad | (upper & (lat == 0)) | (lower & (lat == lats - 1))
    return jnp.where(bad, 0.0, 1.0).astype(F32)


def attend(q_ref, k_ref, v_ref, g, step, keys, with_top, finish):
    units = [(c, h) for j in range(step) for c in range(0, PAD, COLS)
             for h in range(2 * j, 2 * j + 2)]

    def scores(c, h):
        return jnp.dot(k_ref[g * step + h // 2, keys, :], q_ref[g * 2 * step + h, :, c:c + COLS],
                       preferred_element_type=F32)

    def weights(s):
        if with_top:
            s = s - jnp.max(s, axis=0, keepdims=True)
        return jnp.exp2(s).astype(BF16)

    def context(unit, p):
        c, h = unit
        o = jnp.dot(v_ref[g * 2 * step + h, :, keys], p, preferred_element_type=F32)
        finish(g * 2 * step + h, g * step + h // 2, h % 2, slice(c, c + COLS), o)

    s = scores(*units[0])
    held = []
    for n, unit in enumerate(units):
        later = scores(*units[n + 1]) if n + 1 < len(units) else None
        held.append(weights(s))
        if n >= 2:
            context(units[n - 2], held.pop(0))
        s = later
    for unit in units[-2:]:
        context(unit, held.pop(0))


def project_kernel(lats, lons, tok_hbm, w_hbm, qs, ks, vs, early,
                   tok, normed, w, edge, tok_sem, w_sem, send_sem, recv_sem):
    lat, lon = lax.axis_index("lat"), lax.axis_index("lon")
    up, down = lax.rem(lat + lats - 1, lats), lax.rem(lat + 1, lats)
    west, east = lax.rem(lon + lons - 1, lons), lax.rem(lon + 1, lons)
    barrier = pltpu.get_barrier_semaphore()
    around = [(lat, west), (lat, east), (up, lon), (down, lon),
              (up, west), (up, east), (down, west), (down, east)]
    above, below = lat > 0, lat < lats - 1
    there = [None, None, above, below, above, above, below, below]
    behind = [None, None, below, above, below, below, above, above]

    def where_there(condition, action):
        if condition is None:
            action()
        else:
            pl.when(condition)(action)

    for device, condition in zip(around, there):
        where_there(condition, functools.partial(
            pl.semaphore_signal, barrier, inc=1, device_id=device, device_id_type=MESH))

    rows = 320

    def tok_copy(i):
        part = pl.ds(pl.multiple_of(i * rows, rows), rows)
        return pltpu.make_async_copy(tok_hbm.at[part], tok.at[part], tok_sem.at[i])

    for i in range(OWN // rows):
        tok_copy(i).start()

    def w_copy(c):
        at = pl.ds(pl.multiple_of(c * CHUNK, CHUNK), CHUNK)
        return pltpu.make_async_copy(w_hbm.at[:, at], w.at[c], w_sem.at[c])

    for c in range(CHUNKS):
        w_copy(c).start()

    unit = rim_mask(lat, lats, 0, (16, KEYS), 1).astype(BF16)
    for h in range(HEADS):
        other = (1 - h % 2) * HD
        qs[h, other:other + HD, :] = jnp.zeros((HD, PAD), BF16)
        qs[h, h % 2 * HD:h % 2 * HD + HD, OWN:PAD] = jnp.zeros((HD, PAD - OWN), BF16)
        vs[h, HD:HD + 16, :] = unit

    def norm(i, carry):
        tok_copy(i).wait()
        part = pl.ds(pl.multiple_of(i * rows, rows), rows)
        x = tok[part, :].astype(F32)
        centered = x - jnp.mean(x, axis=-1, keepdims=True)
        var = jnp.mean(centered * centered, axis=-1, keepdims=True)
        normed[part, :] = (centered * lax.rsqrt(var + 1e-05)).astype(BF16)
        return carry

    lax.fori_loop(0, OWN // rows, norm, 0)

    take = (picked_rows() == lax.broadcasted_iota(jnp.int32, (2 * SIDE + 4 * CORNER, OWN), 1))
    take = jnp.where(take, 1.0, 0.0).astype(BF16)
    for c in range(2):
        cols = slice(c * 512, c * 512 + 512)
        edge[:, cols] = jnp.dot(take, normed[0:OWN, cols], preferred_element_type=F32).astype(BF16)

    def put_q(y, at):
        t = (y * SCALE).T.astype(BF16)
        for h in range(HEADS):
            low = h % 2 * HD
            qs[h, low:low + HD, at] = t[h * HD:h * HD + HD, :]

    def put_k(y, at):
        y = y.astype(BF16)
        for p in range(PAIRS):
            ks[p, at, :] = y[:, p * 128:p * 128 + 128]

    def put_v(y, at):
        t = y.T.astype(BF16)
        for h in range(HEADS):
            vs[h, 0:HD, at] = t[h * HD:h * HD + HD, :]

    sends = []

    def send():
        pl.semaphore_wait(barrier, 2 + 3 * above.astype(jnp.int32) + 3 * below.astype(jnp.int32))
        e0 = 2 * SIDE
        plan = [
            (edge.at[pl.ds(0, SIDE)], RIGHT, SIDE),
            (edge.at[pl.ds(SIDE, SIDE)], LEFT, SIDE),
            (normed.at[pl.ds(0, CAP)], BOTTOM, CAP),
            (normed.at[pl.ds(OWN - CAP, CAP)], TOP, CAP),
            (edge.at[pl.ds(e0, CORNER)], CORNERS + 3 * CORNER, CORNER),
            (edge.at[pl.ds(e0 + CORNER, CORNER)], CORNERS + 2 * CORNER, CORNER),
            (edge.at[pl.ds(e0 + 2 * CORNER, CORNER)], CORNERS + CORNER, CORNER),
            (edge.at[pl.ds(e0 + 3 * CORNER, CORNER)], CORNERS, CORNER),
        ]
        for n, ((src, at, size), device) in enumerate(zip(plan, around)):
            copy = pltpu.make_async_remote_copy(
                src_ref=src, dst_ref=normed.at[pl.ds(OWN + at, size)],
                send_sem=send_sem.at[n], recv_sem=recv_sem.at[n],
                device_id=device, device_id_type=MESH)
            where_there(there[n], copy.start)
            sends.append(copy)

    for c, put, blocks in ((0, put_q, Q_BLOCKS), (1, put_k, BLOCKS), (2, put_v, BLOCKS)):
        if c == 2:
            send()
        w_copy(c).wait()
        for lo, hi in blocks:
            put(jnp.dot(normed[lo:hi, :], w[c], preferred_element_type=F32), slice(lo, hi))

    def first_keys(g, carry):
        def finish(head, pair, odd, cols, o):
            early[head, :, cols] = o

        attend(qs, ks, vs, g, STEP, slice(0, EARLY), False, finish)
        return carry

    lax.fori_loop(0, PAIRS // STEP, first_keys, 0)

    for n, copy in enumerate(sends):
        where_there(there[n], copy.wait_send)
        where_there(behind[n], copy.wait_recv)

    c0 = CORNERS
    stand = normed[0:CAP, :]
    for lo, hi, at_end in ((TOP, BOTTOM, 0), (c0, c0 + 32, 0),
                           (BOTTOM, c0, lats - 1), (c0 + 32, c0 + 64, lats - 1)):
        def fill(lo=lo, hi=hi):
            normed[OWN + lo:OWN + hi, :] = stand[0:hi - lo]

        pl.when(lat == at_end)(fill)
    mask = rim_mask(lat, lats, FIRST, (KEYS - FIRST, 128))
    mask = jnp.concatenate([mask] * (D // 128), axis=1)
    y = jnp.dot(normed[FIRST:KEYS, :], w[1], preferred_element_type=F32)
    put_k(y, slice(FIRST, KEYS))
    y = jnp.dot(normed[FIRST:KEYS, :], w[2], preferred_element_type=F32)
    put_v(y * mask, slice(FIRST, KEYS))


def attend_kernel(q_ref, k_ref, v_ref, early, tok_hbm, wp_hbm, out_hbm,
                  ctx, tok, wp, out, tok_sem, wp_sem, out_sem):
    tok_copy = pltpu.make_async_copy(tok_hbm, tok, tok_sem)
    wp_copy = pltpu.make_async_copy(wp_hbm, wp, wp_sem)
    tok_copy.start()
    wp_copy.start()

    def run(g, step, with_top):
        state = [jnp.ones((1, COLS), F32), None]

        def finish(head, pair, odd, cols, o):
            if not with_top:
                o = o + early[head, :, cols]
            total = o[HD:HD + 1, :]
            state[0] = jnp.where((total >= SMALL) & (total <= LARGE), state[0], 0.0)
            half = o[0:HD, :] * (1.0 / total)
            if odd:
                ctx[pair, cols, :] = jnp.concatenate([state[1], half], axis=0).T.astype(BF16)
            state[1] = half

        keys = slice(0 if with_top else EARLY, KEYS)
        attend(q_ref, k_ref, v_ref, g, step, keys, with_top, finish)
        return state[0]

    fine = lax.fori_loop(
        0, PAIRS // STEP, lambda g, fine: fine * run(g, STEP, False), jnp.ones((1, COLS), F32))

    @pl.when(jnp.logical_not(jnp.min(fine) > 0.5))
    def _():
        def again(g, carry):
            run(g, 1, True)
            return carry

        lax.fori_loop(0, PAIRS, again, 0)

    tok_copy.wait()
    wp_copy.wait()
    rows = 240
    copies = []
    for n, r in enumerate(range(0, OWN, rows)):
        context = jnp.concatenate([ctx[p, r:r + rows, :] for p in range(PAIRS)], axis=1)
        y = jnp.dot(context, wp[...], preferred_element_type=F32)
        y = y + tok[r:r + rows, :].astype(F32)
        out[r:r + rows, :] = y.astype(BF16)
        part = pl.ds(r, rows)
        copy = pltpu.make_async_copy(out.at[part], out_hbm.at[part], out_sem.at[n])
        copy.start()
        copies.append(copy)
    for copy in copies:
        copy.wait()


def local(lats, lons, tokens, qkv_weight, proj_weight):
    flat = pltpu.with_memory_space_constraint(tokens.reshape(OWN, D), pltpu.HBM)
    any_spec = pl.BlockSpec(memory_space=pl.ANY)
    vm = pltpu.VMEM
    dma = pltpu.SemaphoreType.DMA
    in_vmem = pl.BlockSpec(memory_space=vm)
    results = pl.pallas_call(
        lambda *refs: project_kernel(lats, lons, *refs),
        out_shape=[
            vm((HEADS, 2 * HD, PAD), BF16), vm((PAIRS, KEYS, 128), BF16),
            vm((HEADS, HD + 16, KEYS), BF16), vm((HEADS, HD + 16, PAD), F32),
        ],
        in_specs=[any_spec, any_spec],
        out_specs=[in_vmem] * 4,
        scratch_shapes=[
            vm((OWN, D), BF16), vm((KEYS, D), BF16), vm((CHUNKS, D, CHUNK), BF16),
            vm((2 * SIDE + 4 * CORNER, D), BF16),
            dma((OWN // 320,)), dma((CHUNKS,)), dma((8,)), dma((8,)),
        ],
        compiler_params=pltpu.CompilerParams(
            collective_id=0, has_side_effects=True, vmem_limit_bytes=40 * 2 ** 20),
    )(flat, qkv_weight)
    results = [pltpu.with_memory_space_constraint(x, vm) for x in results]
    mixed = pl.pallas_call(
        attend_kernel,
        out_shape=jax.ShapeDtypeStruct((OWN, D), BF16),
        in_specs=[in_vmem] * 4 + [any_spec] * 2,
        out_specs=any_spec,
        scratch_shapes=[
            vm((PAIRS, PAD, 128), BF16), vm((OWN, D), BF16), vm((D, D), BF16),
            vm((OWN, D), BF16), dma(()), dma(()), dma((4,)),
        ],
        compiler_params=pltpu.CompilerParams(vmem_limit_bytes=40 * 2 ** 20),
    )(*results, flat, proj_weight)
    return mixed.reshape(TH, TW, D)


def solution(mesh):
    lats, lons = mesh.shape["lat"], mesh.shape["lon"]
    return jax.shard_map(
        lambda *args: local(lats, lons, *args), mesh=mesh,
        in_specs=(P("lat", "lon", None), P(), P()), out_specs=P("lat", "lon", None),
        check_vma=False)
```
